32 devices in a mesh: row: 8 (over z, x), col: 4 (over y, core).
Axes of the slice: x: 2, y: 2, z: 4, core: 2. Of those that a mesh axis runs over, the one named last changes fastest.
Arguments:
- object_field: float32 [4, 2, 1024, 512], P(None, None, 'row', 'col'), may hold values from -5 to 5
- probe_wave: float32 [2, 128, 128], replicated, may hold values from -6 to 6
- positions: int32 [8, 4, 2, 2], P('row', 'col'), may hold values from 0 to 1023, as said below
- counts: int32 [8, 4], P('row', 'col'), may hold values from 0 to 2, as said below
- measured: float32 [8, 4, 2, 128, 128], P('row', 'col'), may hold values from 0 to 2
Outputs:
- object_grad: float32 [4, 2, 1024, 512], P(None, None, 'row', 'col')
- probe_grad: float32 [2, 128, 128], replicated
The draws below stay inside these ranges and needn't reach their ends.
Inputs may be any that keep to these rules, and one draw needn't show every extreme that they name: positions[r, c, s] lies inside tile (r, c): its row in r * 128 to (r + 1) * 128 - 1 and its column in c * 128 to (c + 1) * 128 - 1; dead slots hold such positions too. `counts`: some tile has 2 live slots.
All inputs are finite; a program needn't handle non-finite values.
Results may differ from the reference program's by a relative error of at most 0.0003.
Values sent between devices are 32-bit elements; how exact they have to be, the bound alone decides.
A program may use at most 64 MiB of HBM per device.

```python
import math
import jax
import jax.numpy as jnp
from jax import lax

TR = 128
TC = 128
PROBE = 128
SLICES = 4
CAP = 2
GRID_ROWS = 8
GRID_COLS = 4
NR = 1024
NC = 512


def draw_positions(key, part):
    row_key = jax.random.fold_in(key, 11)
    col_key = jax.random.fold_in(key, 12)
    shape_all = (GRID_ROWS, GRID_COLS, CAP)
    offset_rows = jax.random.randint(row_key, shape_all, 0, TR)
    offset_cols = jax.random.randint(col_key, shape_all, 0, TC)
    tile_row = lax.broadcasted_iota(jnp.int32, shape_all, 0)
    tile_col = lax.broadcasted_iota(jnp.int32, shape_all, 1)
    centre_rows = tile_row * TR + offset_rows
    centre_cols = tile_col * TC + offset_cols
    return jnp.stack([centre_rows, centre_cols], axis=-1).astype(jnp.int32)


def draw_counts(key, part):
    base_key = jax.random.fold_in(key, 21)
    pick_key = jax.random.fold_in(key, 22)
    drawn = jax.random.randint(base_key, (GRID_ROWS, GRID_COLS), 0, CAP + 1)
    chosen = jax.random.randint(pick_key, (), 0, GRID_ROWS * GRID_COLS)
    flat_index = lax.broadcasted_iota(jnp.int32, (GRID_ROWS, GRID_COLS), 0) * GRID_COLS + lax.broadcasted_iota(jnp.int32, (GRID_ROWS, GRID_COLS), 1)
    return jnp.where(flat_index == chosen, CAP, drawn).astype(jnp.int32)


def shard_levels(rng, shape, shards, smallest, largest):
    factor_of, own = 1.0, jax.random.fold_in(rng, 6)
    for dim, parts in shards:
        steps = jnp.exp(jax.random.uniform(jax.random.fold_in(own, dim), (parts,), jnp.float32, smallest / len(shards), largest / len(shards)))
        factor_of = factor_of * jnp.repeat(steps, shape[dim] // parts).reshape([-1 if axis == dim else 1 for axis in range(len(shape))])
    return factor_of


def bell_draw(rng, extent, width, limit, cuts=(), kind=jnp.bfloat16):
    values = jax.random.normal(rng, extent, jnp.float32) * width
    if len(cuts) > 0:
        values = shard_levels(rng, extent, cuts, -0.22, 0.18) * values
    return jnp.clip(values, min=-limit, max=limit).astype(kind)


def setup_inputs(seed: int = 0) -> dict:
    key_of = jax.random.split(jax.random.key(seed), 6)
    object_field = bell_draw(key_of[0], (SLICES, 2, NR, NC), 0.7, 5.0, ((2, 8), (3, 4)), jnp.float32)
    probe_wave = bell_draw(key_of[1], (2, PROBE, PROBE), 1.0, 6.0, (), jnp.float32)
    positions = draw_positions(jax.random.fold_in(key_of[5], 71), 0)
    counts = draw_counts(jax.random.fold_in(key_of[5], 71), 0)
    measured = jnp.clip(2.0 * jax.random.uniform(key_of[4], (GRID_ROWS, GRID_COLS, CAP, PROBE, PROBE), jnp.float32) ** shard_levels(key_of[4], (GRID_ROWS, GRID_COLS, CAP, PROBE, PROBE), ((0, 8), (1, 4)), -0.2, 0.2), 0.0, 2.0)
    return {"object_field": object_field, "probe_wave": probe_wave, "positions": positions, "counts": counts, "measured": measured}


FRESNEL = 0.01

def matmul_exact(left, right):
    return jnp.dot(left, right, precision=lax.Precision.HIGHEST, preferred_element_type=jnp.float32)

def complex_matmul(left_real, left_imag, right_real, right_imag):
    real_out = matmul_exact(left_real, right_real) - matmul_exact(left_imag, right_imag)
    imag_out = matmul_exact(left_real, right_imag) + matmul_exact(left_imag, right_real)
    return (real_out, imag_out)

def transform(real_part, imag_part, table_real, table_imag):
    first_real, first_imag = complex_matmul(table_real, table_imag, real_part, imag_part)
    return complex_matmul(first_real, first_imag, table_real, table_imag)

def make_tables(points):
    indices = jnp.arange(points, dtype=jnp.int32)
    product = indices[:, None] * indices[None, :] % points
    phase_angle = 2.0 * math.pi / points * product.astype(jnp.float32)
    norm_scale = 1.0 / math.sqrt(points)
    table_real = jnp.cos(phase_angle) * norm_scale
    table_imag = -jnp.sin(phase_angle) * norm_scale
    frequency = jnp.where(indices < points // 2, indices, indices - points).astype(jnp.float32)
    prop_phase = -FRESNEL * (frequency[:, None] ** 2 + frequency[None, :] ** 2)
    return (table_real, table_imag, jnp.cos(prop_phase), jnp.sin(prop_phase))

def position_loss(patch_stack, probe_wave, measured_one, tables):
    table_real, table_imag, prop_real, prop_imag = tables
    wave_real = probe_wave[0]
    wave_imag = probe_wave[1]
    slice_count = patch_stack.shape[0]
    for depth_index in range(slice_count):
        trans_real = patch_stack[depth_index, 0]
        trans_imag = patch_stack[depth_index, 1]
        exit_real = wave_real * trans_real - wave_imag * trans_imag
        exit_imag = wave_real * trans_imag + wave_imag * trans_real
        far_real, far_imag = transform(exit_real, exit_imag, table_real, table_imag)
        if depth_index + 1 < slice_count:
            moved_real = far_real * prop_real - far_imag * prop_imag
            moved_imag = far_real * prop_imag + far_imag * prop_real
            wave_real, wave_imag = transform(moved_real, moved_imag, table_real, -table_imag)
    amplitude = jnp.sqrt(far_real * far_real + far_imag * far_imag + 1.0)
    return jnp.sum((amplitude - measured_one) ** 2)

def reference(object_field, probe_wave, positions, counts, measured):
    slice_count = object_field.shape[0]
    probe_size = probe_wave.shape[-1]
    half_probe = probe_size // 2
    tables = make_tables(probe_size)
    padded = jnp.pad(object_field, ((0, 0), (0, 0), (half_probe, half_probe), (half_probe, half_probe)))
    slot_count = positions.shape[2]
    live_mask = (jnp.arange(slot_count, dtype=jnp.int32)[None, None, :] < counts[:, :, None]).reshape(-1)
    centres = positions.reshape(-1, 2)
    patterns = measured.reshape(-1, probe_size, probe_size)
    gradient = jax.grad(position_loss, argnums=(0, 1))
    anchor = jnp.zeros((), jnp.int32)

    def visit(state_pair, scan_item):
        object_sum, probe_sum = state_pair
        centre, is_live, pattern = scan_item
        starts = (anchor, anchor, centre[0].astype(jnp.int32), centre[1].astype(jnp.int32))
        patch_stack = lax.dynamic_slice(padded, starts, (slice_count, 2, probe_size, probe_size))
        patch_grad, wave_grad = gradient(patch_stack, probe_wave, pattern, tables)
        weight = is_live.astype(jnp.float32)
        current = lax.dynamic_slice(object_sum, starts, (slice_count, 2, probe_size, probe_size))
        object_sum = lax.dynamic_update_slice(object_sum, current + weight * patch_grad, starts)
        return ((object_sum, probe_sum + weight * wave_grad), 0)
    initial = (jnp.zeros(padded.shape, jnp.float32), jnp.zeros(probe_wave.shape, jnp.float32))
    final_pair, unused = lax.scan(visit, initial, (centres, live_mask, patterns))
    object_sum, probe_sum = final_pair
    object_grad = object_sum[:, :, half_probe:-half_probe, half_probe:-half_probe]
    return (object_grad, probe_sum)
```

```python
import functools
import math

import jax
import jax.numpy as jnp
import numpy as np
from jax import lax
from jax.experimental import pallas as pl
from jax.experimental.pallas import tpu as pltpu
from jax.sharding import PartitionSpec as P

FRESNEL = 0.01
MESH = pl.DeviceIdType.MESH


def tables(points):
    index = np.arange(points)
    dft = np.exp(-2j * math.pi * ((index[:, None] * index[None, :]) % points) / points) / math.sqrt(points)
    freq = np.where(index < points // 2, index, index - points).astype(np.float64)
    step = np.conj(dft) @ (np.exp(-1j * FRESNEL * freq**2)[:, None] * dft)
    blocks = []
    for m in (step, dft):
        right = np.block([[m.real, m.imag], [-m.imag, m.real]])
        left = np.block([[m.real, -m.imag], [m.imag, m.real]])
        blocks += [right, left]
    full = np.stack(blocks).astype(np.float32)
    high = full.astype(jnp.bfloat16)
    low = (full - high.astype(np.float32)).astype(jnp.bfloat16)
    return np.stack([high, low], axis=1)


def split(x):
    high = x.astype(jnp.bfloat16)
    return high, (x - high.astype(jnp.float32)).astype(jnp.bfloat16)


def dot(a, b):
    return jnp.dot(a, b, preferred_element_type=jnp.float32)


def kernel(R, C, pos, cnt, obj, probe, meas, mats, out, pg_out,
           row_in, col_send, col_in, padded, patch, wave, zpad, g_send, g_in, m_send, m_in,
           pg, s1, q1, s2, q2, f2,
           hs_sem, hr_sem, as_sem, ar_sem, bs_sem, br_sem):
    K = obj.shape[0]
    N = obj.shape[-1]
    H = N // 2
    S = meas.shape[2]
    r = lax.axis_index("row")
    c = lax.axis_index("col")

    barrier = pltpu.get_barrier_semaphore()
    for j in range(1, R):
        pl.semaphore_signal(barrier, inc=1, device_id=(lax.rem(r + j, R), c), device_id_type=MESH)
    for j in range(1, C):
        pl.semaphore_signal(barrier, inc=1, device_id=(r, lax.rem(c + j, C)), device_id_type=MESH)
    pl.semaphore_wait(barrier, R + C - 2)

    have = {"up": r > 0, "down": r < R - 1, "left": c > 0, "right": c < C - 1}
    where_to = {"up": (r - 1, c), "down": (r + 1, c), "left": (r, c - 1), "right": (r, c + 1)}
    back = {"up": "down", "down": "up", "left": "right", "right": "left"}
    slot = {"up": 0, "down": 1, "left": 0, "right": 1}

    def row_refs(k, side):
        rows = pl.ds(0, H) if side == "up" else pl.ds(H, H)
        return obj.at[k, :, rows, :], row_in.at[k, slot[back[side]]]

    def own_refs(k, side):
        return col_send.at[k, slot[side], 0], col_in.at[k, slot[back[side]], 0]

    def halo_refs(k, side):
        return col_send.at[k, slot[side], 1], col_in.at[k, slot[back[side]], 1]

    def gcol_refs(k, side):
        return g_send.at[k, slot[side]], g_in.at[k, slot[back[side]]]

    def grow_refs(k, side):
        return m_send.at[k, slot[side]], m_in.at[k, slot[back[side]]]

    kinds = {"row": (0, row_refs, ("up", "down")), "own": (1, own_refs, ("left", "right")),
             "halo": (2, halo_refs, ("left", "right")), "gcol": (3, gcol_refs, ("left", "right")),
             "grow": (4, grow_refs, ("up", "down"))}

    def copy_to(kind, k, side):
        number, refs, _ = kinds[kind]
        src, dst = refs(k, side)
        return pltpu.make_async_remote_copy(
            src_ref=src, dst_ref=dst,
            send_sem=hs_sem.at[number, k, slot[side]],
            recv_sem=hr_sem.at[number, k, slot[back[side]]],
            device_id=where_to[side], device_id_type=MESH)

    def send(kind, k):
        for side in kinds[kind][2]:
            @pl.when(have[side])
            def _():
                copy_to(kind, k, side).start()

    def receive(kind, k):
        for side in kinds[kind][2]:
            @pl.when(have[side])
            def _():
                number, refs, _ = kinds[kind]
                src, dst = refs(k, back[side])
                pltpu.make_async_remote_copy(
                    src_ref=src, dst_ref=dst,
                    send_sem=hs_sem.at[number, k, slot[back[side]]],
                    recv_sem=hr_sem.at[number, k, slot[side]],
                    device_id=where_to[side], device_id_type=MESH).wait_recv()

    def sent(kind, k):
        for side in kinds[kind][2]:
            @pl.when(have[side])
            def _():
                copy_to(kind, k, side).wait_send()

    lane = lax.broadcasted_iota(jnp.int32, (N, N), 1)
    low = lane < H
    low_h = lane[:H] < H

    def turn(x):
        return pltpu.roll(x, H, 1)

    for k in range(K):
        send("row", k)
    for k in range(K):
        re, im = obj[k, 0], obj[k, 1]
        col_send[k, 0, 0] = jnp.where(low, re, turn(im))
        col_send[k, 1, 0] = jnp.where(low, turn(re), im)
        send("own", k)

    for side, buffers in (("up", (row_in, m_in)), ("down", (row_in, m_in)),
                          ("left", (col_in, g_in)), ("right", (col_in, g_in))):
        @pl.when(jnp.logical_not(have[side]))
        def _():
            for buffer in buffers:
                for k in range(K):
                    buffer[k, slot[side]] = jnp.zeros(buffer.shape[2:], jnp.float32)
    for s in range(S):
        for p in range(2):
            zpad[s, p, :, pl.ds(0, N), :] = jnp.zeros((2, N, N), jnp.float32)
            zpad[s, p, :, pl.ds(2 * N, N), :] = jnp.zeros((2, N, N), jnp.float32)

    ys = [jnp.clip(pos[0, 0, s, 0] - r * N, 0, N - 1) for s in range(S)]
    xs = [jnp.clip(pos[0, 0, s, 1] - c * N, 0, N - 1) for s in range(S)]
    live = [(s < cnt[0, 0]).astype(jnp.float32) for s in range(S)]

    def forward_halo(k):
        receive("row", k)
        for d in range(2):
            re, im = row_in[k, d, 0], row_in[k, d, 1]
            rows = pl.ds(d * H, H)
            col_send[k, 0, 1, rows, :] = jnp.where(low_h, re, turn(im))
            col_send[k, 1, 1, rows, :] = jnp.where(low_h, turn(re), im)
        send("halo", k)

    def assemble(k):
        receive("own", k)
        receive("halo", k)
        for start, size, mid, part, begin in (
                (0, H, lambda p: row_in[k, 0, p], 1, 0),
                (H, N, lambda p: obj[k, p], 0, 0),
                (H + N, H, lambda p: row_in[k, 1, p], 1, H)):
            left = col_in[k, 0, part, pl.ds(begin, size), :]
            right = col_in[k, 1, part, pl.ds(begin, size), :]
            mask = low if size == N else low_h
            re, im = mid(0), mid(1)
            rows = pl.ds(start, size)
            padded[k, 0, 0, rows, :] = jnp.where(mask, left, turn(re))
            padded[k, 0, 1, rows, :] = turn(jnp.where(mask, right, re))
            padded[k, 1, 0, rows, :] = turn(jnp.where(mask, im, left))
            padded[k, 1, 1, rows, :] = jnp.where(mask, turn(im), right)

    def window(k, s, p):
        rows = pl.ds(ys[s], N)
        shift = lax.rem(N - xs[s], N)
        first = pltpu.roll(padded[k, p, 0, rows, :], shift, 1)
        second = pltpu.roll(padded[k, p, 1, rows, :], shift, 1)
        return jnp.where(lane < N - xs[s], first, second)

    def sandwich(res, ims, right, left):
        x = jnp.concatenate([jnp.concatenate([a, b], axis=1) for a, b in zip(res, ims)], axis=0)
        xh, xl = split(x)
        mh, ml = mats[right, 0], mats[right, 1]
        y = dot(xh, mh) + (dot(xl, mh) + dot(xh, ml))
        y = jnp.concatenate(
            [jnp.concatenate([y[s * N:(s + 1) * N, :N] for s in range(S)], axis=1),
             jnp.concatenate([y[s * N:(s + 1) * N, N:] for s in range(S)], axis=1)], axis=0)
        yh, yl = split(y)
        mh, ml = mats[left, 0], mats[left, 1]
        z = dot(mh, yh) + (dot(mh, yl) + dot(ml, yh))
        return ([z[:N, s * N:(s + 1) * N] for s in range(S)],
                [z[N:, s * N:(s + 1) * N] for s in range(S)])

    forward_halo(0)
    for k in range(K):
        assemble(k)
        if k + 1 < K:
            forward_halo(k + 1)
        exit_re, exit_im = [], []
        for s in range(S):
            tr, ti = window(k, s, 0), window(k, s, 1)
            patch[k, s, 0] = tr
            patch[k, s, 1] = ti
            if k == 0:
                wr, wi = probe[0], probe[1]
            else:
                wr, wi = wave[k - 1, s, 0], wave[k - 1, s, 1]
            exit_re.append(wr * tr - wi * ti)
            exit_im.append(wr * ti + wi * tr)
        if k + 1 < K:
            next_re, next_im = sandwich(exit_re, exit_im, 0, 1)
            for s in range(S):
                wave[k, s, 0] = next_re[s]
                wave[k, s, 1] = next_im[s]
        else:
            far_re, far_im = sandwich(exit_re, exit_im, 2, 3)

    grad_re, grad_im = [], []
    for s in range(S):
        amplitude = jnp.sqrt(far_re[s] * far_re[s] + far_im[s] * far_im[s] + 1.0)
        factor = (2.0 * live[s]) * (amplitude - meas[0, 0, s]) / amplitude
        grad_re.append(factor * far_re[s])
        grad_im.append(factor * far_im[s])

    def fold_columns(k):
        receive("gcol", k)
        left, right = g_in[k, 0], g_in[k, 1]
        mask = jnp.concatenate([low, low], axis=0)
        add_re = jnp.where(mask, left, turn(right))
        add_im = jnp.where(mask, turn(left), right)
        for p, add in ((0, add_re), (1, add_im)):
            total = padded[k, p, 0] + add
            m_send[k, 0, p] = total[:H]
            m_send[k, 1, p] = total[H + N:]
            out[k, p] = total[H:H + N]
        send("grow", k)

    for k in range(K - 1, -1, -1):
        right, left = (3, 2) if k == K - 1 else (1, 0)
        ge_re, ge_im = sandwich(grad_re, grad_im, right, left)
        for s in range(S):
            if k == 0:
                wr, wi = probe[0], probe[1]
            else:
                wr, wi = wave[k - 1, s, 0], wave[k - 1, s, 1]
            parts = (wr * ge_re[s] + wi * ge_im[s], wr * ge_im[s] - wi * ge_re[s])
            for p in range(2):
                moved = pltpu.roll(parts[p], xs[s], 1)
                zpad[s, p, 0, pl.ds(N, N), :] = jnp.where(lane >= xs[s], moved, 0.0)
                zpad[s, p, 1, pl.ds(N, N), :] = jnp.where(lane < xs[s], moved, 0.0)
        halves = []
        for p in range(2):
            halves.append([sum(zpad[s, p, h, pl.ds(N - ys[s], 2 * N), :] for s in range(S))
                           for h in range(2)])
        (re_lo, re_hi), (im_lo, im_hi) = halves
        mask = jnp.concatenate([low, low], axis=0)
        g_send[k, 0] = jnp.where(mask, re_lo, turn(im_lo))
        g_send[k, 1] = jnp.where(mask, turn(re_hi), im_hi)
        send("gcol", k)
        padded[k, 0, 0] = turn(jnp.where(mask, re_hi, re_lo))
        padded[k, 1, 0] = turn(jnp.where(mask, im_hi, im_lo))
        new_re, new_im = [], []
        for s in range(S):
            tr, ti = patch[k, s, 0], patch[k, s, 1]
            new_re.append(tr * ge_re[s] + ti * ge_im[s])
            new_im.append(tr * ge_im[s] - ti * ge_re[s])
        grad_re, grad_im = new_re, new_im
        if k + 1 < K:
            fold_columns(k + 1)

    pg[pl.ds(0, N), :] = sum(grad_re)
    pg[pl.ds(N, N), :] = sum(grad_im)
    h1 = 2 * N // C
    owners = min(R, h1 // 8)
    h2 = h1 // owners

    def piece(index, size):
        return pl.ds(pl.multiple_of(index * size, 8), size)

    def exchange(me, peer, src, dst, send_sem, recv_sem, device):
        return pltpu.make_async_remote_copy(
            src_ref=src, dst_ref=dst, send_sem=send_sem.at[peer], recv_sem=recv_sem.at[me],
            device_id=device, device_id_type=MESH)

    def col_scatter(me, peer):
        return exchange(me, peer, pg.at[piece(peer, h1)], s1.at[me], as_sem.at[0], ar_sem.at[0], (r, peer))

    def row_scatter(me, peer):
        return exchange(me, peer, q1.at[piece(peer, h2)], s2.at[me], bs_sem.at[0], br_sem.at[0], (peer, c))

    def row_gather(me, peer):
        return exchange(me, peer, q2, f2.at[piece(me, h2)], bs_sem.at[1], br_sem.at[1], (peer, c))

    def col_gather(me, peer):
        return exchange(me, peer, f2, pg_out.at[piece(me, h1)], as_sem.at[1], ar_sem.at[1], (r, peer))

    def when_owner(index, action):
        if owners == R:
            action()
        else:
            pl.when(index < owners)(action)

    col_peers = [lax.rem(c + j, C) for j in range(1, C)]
    row_peers = [lax.rem(r + j, R) for j in range(1, R)]

    for peer in col_peers:
        col_scatter(c, peer).start()
    fold_columns(0)
    s1[c] = pg[piece(c, h1), :]
    for peer in col_peers:
        col_scatter(peer, c).wait_recv()
    q1[...] = sum(s1[j] for j in range(C))
    for peer in row_peers:
        when_owner(peer, lambda: row_scatter(r, peer).start())

    def reduce_rows():
        s2[r] = q1[piece(r, h2), :]
        for peer in row_peers:
            row_scatter(peer, r).wait_recv()
        total = sum(s2[j] for j in range(R))
        q2[...] = total
        f2[piece(r, h2), :] = total
        for peer in row_peers:
            row_gather(r, peer).start()

    when_owner(r, reduce_rows)
    for peer in row_peers:
        when_owner(peer, lambda: row_gather(peer, r).wait_recv())
    for peer in col_peers:
        col_gather(c, peer).start()
    pg_out[piece(c, h1), :] = f2[...]

    for k in range(K - 1, -1, -1):
        receive("grow", k)
        for p in range(2):
            out[k, p, pl.ds(0, H), :] += m_in[k, 0, p]
            out[k, p, pl.ds(H, H), :] += m_in[k, 1, p]

    for peer in col_peers:
        col_gather(peer, c).wait_recv()
    for kind in kinds:
        for k in range(K):
            sent(kind, k)
    for peer in col_peers:
        col_scatter(c, peer).wait_send()
        col_gather(c, peer).wait_send()
    for peer in row_peers:
        when_owner(peer, lambda: row_scatter(r, peer).wait_send())
    for peer in row_peers:
        when_owner(r, lambda: row_gather(r, peer).wait_send())


def per_device(R, C, object_field, probe_wave, positions, counts, measured):
    K, _, N, _ = object_field.shape
    S = measured.shape[2]
    H = N // 2
    f32 = jnp.float32
    h1 = 2 * N // C
    owners = min(R, h1 // 8)
    h2 = h1 // owners
    vmem = pl.BlockSpec(memory_space=pltpu.VMEM)
    smem = pl.BlockSpec(memory_space=pltpu.SMEM)
    dma = pltpu.SemaphoreType.DMA
    grad, probe_grad = pl.pallas_call(
        functools.partial(kernel, R, C),
        out_shape=(jax.ShapeDtypeStruct(object_field.shape, f32), jax.ShapeDtypeStruct((2 * N, N), f32)),
        in_specs=[smem, smem, vmem, vmem, vmem, vmem],
        out_specs=(vmem, vmem),
        scratch_shapes=[
            pltpu.VMEM((K, 2, 2, H, N), f32),
            pltpu.VMEM((K, 2, 2, N, N), f32),
            pltpu.VMEM((K, 2, 2, N, N), f32),
            pltpu.VMEM((K, 2, 2, 2 * N, N), f32),
            pltpu.VMEM((K, S, 2, N, N), f32),
            pltpu.VMEM((K - 1, S, 2, N, N), f32),
            pltpu.VMEM((S, 2, 2, 3 * N, N), f32),
            pltpu.VMEM((K, 2, 2 * N, N), f32),
            pltpu.VMEM((K, 2, 2 * N, N), f32),
            pltpu.VMEM((K, 2, 2, H, N), f32),
            pltpu.VMEM((K, 2, 2, H, N), f32),
            pltpu.VMEM((2 * N, N), f32),
            pltpu.VMEM((C, h1, N), f32),
            pltpu.VMEM((h1, N), f32),
            pltpu.VMEM((R, h2, N), f32),
            pltpu.VMEM((h2, N), f32),
            pltpu.VMEM((h1, N), f32),
            dma((5, K, 2)), dma((5, K, 2)),
            dma((2, C)), dma((2, C)),
            dma((2, R)), dma((2, R)),
        ],
        compiler_params=pltpu.CompilerParams(
            collective_id=0, has_side_effects=True, vmem_limit_bytes=40 * 1024 * 1024),
    )(positions, counts, object_field, probe_wave, measured, jnp.asarray(tables(N)))
    return grad, probe_grad.reshape(2, N, N)


def solution(mesh):
    in_specs = (
        P(None, None, "row", "col"),
        P(),
        P("row", "col", None, None),
        P("row", "col"),
        P("row", "col", None, None, None),
    )
    out_specs = (P(None, None, "row", "col"), P())
    body = functools.partial(per_device, mesh.shape["row"], mesh.shape["col"])
    return jax.shard_map(body, mesh=mesh, in_specs=in_specs, out_specs=out_specs, check_vma=False)
```

```python
import functools
import math

import jax
import jax.numpy as jnp
import numpy as np
from jax import lax
from jax.experimental import pallas as pl
from jax.experimental.pallas import tpu as pltpu
from jax.sharding import PartitionSpec as P

FRESNEL = 0.01
MESH = pl.DeviceIdType.MESH


def tables(points):
    index = np.arange(points)
    dft = np.exp(-2j * math.pi * ((index[:, None] * index[None, :]) % points) / points) / math.sqrt(points)
    freq = np.where(index < points // 2, index, index - points).astype(np.float64)
    step = np.conj(dft) @ (np.exp(-1j * FRESNEL * freq**2)[:, None] * dft)
    blocks = []
    for m in (step, dft):
        right = np.block([[m.real, m.imag], [-m.imag, m.real]])
        left = np.block([[m.real, -m.imag], [m.imag, m.real]])
        blocks += [right, left]
    full = np.stack(blocks).astype(np.float32)
    high = full.astype(jnp.bfloat16)
    low = (full - high.astype(np.float32)).astype(jnp.bfloat16)
    return np.stack([high, low], axis=1)


def split(x):
    high = x.astype(jnp.bfloat16)
    return high, (x - high.astype(jnp.float32)).astype(jnp.bfloat16)


def dot(a, b):
    return jnp.dot(a, b, preferred_element_type=jnp.float32)


def kernel(R, C, pos, cnt, obj_h, probe_h, meas_h, mats_h, out, pg_out,
           obj, probe, meas, mats,
           row_in, col_send, col_in, padded, patch, wave, zpad, g_send, g_in, m_send, m_in,
           pg, s1, q1, s2, q2, f2,
           hs_sem, hr_sem, as_sem, ar_sem, bs_sem, br_sem, local_sem):
    K = obj_h.shape[0]
    N = obj_h.shape[-1]
    H = N // 2
    S = meas.shape[2]
    r = lax.axis_index("row")
    c = lax.axis_index("col")

    barrier = pltpu.get_barrier_semaphore()
    for j in range(1, R):
        pl.semaphore_signal(barrier, inc=1, device_id=(lax.rem(r + j, R), c), device_id_type=MESH)
    for j in range(1, C):
        pl.semaphore_signal(barrier, inc=1, device_id=(r, lax.rem(c + j, C)), device_id_type=MESH)

    fetch_obj = [pltpu.make_async_copy(obj_h.at[k], obj.at[k], local_sem.at[k]) for k in range(K)]
    fetch_probe = pltpu.make_async_copy(probe_h, probe, local_sem.at[K])
    fetch_meas = pltpu.make_async_copy(meas_h, meas, local_sem.at[K + 1])
    fetch_mats = [pltpu.make_async_copy(mats_h.at[i], mats.at[i], local_sem.at[K + 2 + i]) for i in range(4)]
    for fetch in fetch_obj + [fetch_probe] + fetch_mats + [fetch_meas]:
        fetch.start()

    have = {"up": r > 0, "down": r < R - 1, "left": c > 0, "right": c < C - 1}
    where_to = {"up": (r - 1, c), "down": (r + 1, c), "left": (r, c - 1), "right": (r, c + 1)}
    back = {"up": "down", "down": "up", "left": "right", "right": "left"}
    slot = {"up": 0, "down": 1, "left": 0, "right": 1}

    def row_refs(k, side):
        rows = pl.ds(0, H) if side == "up" else pl.ds(H, H)
        return obj_h.at[k, :, rows, :], row_in.at[k, slot[back[side]]]

    def own_refs(k, side):
        return col_send.at[k, slot[side], 0], col_in.at[k, slot[back[side]], 0]

    def halo_refs(k, side):
        return col_send.at[k, slot[side], 1], col_in.at[k, slot[back[side]], 1]

    def gcol_refs(k, side):
        return g_send.at[k, slot[side]], g_in.at[k, slot[back[side]]]

    def grow_refs(k, side):
        return m_send.at[k, slot[side]], m_in.at[k, slot[back[side]]]

    kinds = {"row": (0, row_refs, ("up", "down")), "own": (1, own_refs, ("left", "right")),
             "halo": (2, halo_refs, ("left", "right")), "gcol": (3, gcol_refs, ("left", "right")),
             "grow": (4, grow_refs, ("up", "down"))}

    def copy_to(kind, k, side):
        number, refs, _ = kinds[kind]
        src, dst = refs(k, side)
        return pltpu.make_async_remote_copy(
            src_ref=src, dst_ref=dst,
            send_sem=hs_sem.at[number, k, slot[side]],
            recv_sem=hr_sem.at[number, k, slot[back[side]]],
            device_id=where_to[side], device_id_type=MESH)

    def send(kind, k):
        for side in kinds[kind][2]:
            @pl.when(have[side])
            def _():
                copy_to(kind, k, side).start()

    def receive(kind, k):
        for side in kinds[kind][2]:
            @pl.when(have[side])
            def _():
                number, refs, _ = kinds[kind]
                src, dst = refs(k, back[side])
                pltpu.make_async_remote_copy(
                    src_ref=src, dst_ref=dst,
                    send_sem=hs_sem.at[number, k, slot[back[side]]],
                    recv_sem=hr_sem.at[number, k, slot[side]],
                    device_id=where_to[side], device_id_type=MESH).wait_recv()

    def sent():
        for side in have:
            @pl.when(have[side])
            def _():
                for kind in kinds:
                    if side in kinds[kind][2]:
                        for k in range(K):
                            copy_to(kind, k, side).wait_send()

    lane = lax.broadcasted_iota(jnp.int32, (N, N), 1)
    low = lane < H
    low_h = lane[:H] < H

    def turn(x):
        return pltpu.roll(x, H, 1)

    for side, buffers in (("up", (row_in, m_in)), ("down", (row_in, m_in)),
                          ("left", (col_in, g_in)), ("right", (col_in, g_in))):
        @pl.when(jnp.logical_not(have[side]))
        def _():
            for buffer in buffers:
                for k in range(K):
                    buffer[k, slot[side]] = jnp.zeros(buffer.shape[2:], jnp.float32)
    for s in range(S):
        for p in range(2):
            zpad[s, p, :, pl.ds(0, N), :] = jnp.zeros((2, N, N), jnp.float32)
            zpad[s, p, :, pl.ds(2 * N, N), :] = jnp.zeros((2, N, N), jnp.float32)

    pl.semaphore_wait(barrier, R + C - 2)

    def pack_own(k):
        fetch_obj[k].wait()
        re, im = obj[k, 0], obj[k, 1]
        col_send[k, 0, 0] = jnp.where(low, re, turn(im))
        col_send[k, 1, 0] = jnp.where(low, turn(re), im)
        send("own", k)

    send("row", 0)
    pack_own(0)
    send("row", 1)
    pack_own(1)

    ys = [jnp.clip(pos[0, 0, s, 0] - r * N, 0, N - 1) for s in range(S)]
    xs = [jnp.clip(pos[0, 0, s, 1] - c * N, 0, N - 1) for s in range(S)]
    live = [(s < cnt[0, 0]).astype(jnp.float32) for s in range(S)]

    def forward_halo(k):
        receive("row", k)
        for d in range(2):
            re, im = row_in[k, d, 0], row_in[k, d, 1]
            rows = pl.ds(d * H, H)
            col_send[k, 0, 1, rows, :] = jnp.where(low_h, re, turn(im))
            col_send[k, 1, 1, rows, :] = jnp.where(low_h, turn(re), im)
        send("halo", k)
        if k + 2 < K:
            send("row", k + 2)
            pack_own(k + 2)

    def assemble(k):
        receive("own", k)
        receive("halo", k)
        for start, size, mid, part, begin in (
                (0, H, lambda p: row_in[k, 0, p], 1, 0),
                (H, N, lambda p: obj[k, p], 0, 0),
                (H + N, H, lambda p: row_in[k, 1, p], 1, H)):
            left = col_in[k, 0, part, pl.ds(begin, size), :]
            right = col_in[k, 1, part, pl.ds(begin, size), :]
            mask = low if size == N else low_h
            re, im = mid(0), mid(1)
            rows = pl.ds(start, size)
            padded[k, 0, 0, rows, :] = jnp.where(mask, left, turn(re))
            padded[k, 0, 1, rows, :] = turn(jnp.where(mask, right, re))
            padded[k, 1, 0, rows, :] = turn(jnp.where(mask, im, left))
            padded[k, 1, 1, rows, :] = jnp.where(mask, turn(im), right)

    def window(k, s, p):
        rows = pl.ds(ys[s], N)
        shift = lax.rem(N - xs[s], N)
        first = pltpu.roll(padded[k, p, 0, rows, :], shift, 1)
        second = pltpu.roll(padded[k, p, 1, rows, :], shift, 1)
        return jnp.where(lane < N - xs[s], first, second)

    def sandwich(res, ims, right, left):
        x = jnp.concatenate([jnp.concatenate([a, b], axis=1) for a, b in zip(res, ims)], axis=0)
        xh, xl = split(x)
        mh, ml = mats[right, 0], mats[right, 1]
        y = dot(xh, mh) + (dot(xl, mh) + dot(xh, ml))
        y = jnp.concatenate(
            [jnp.concatenate([y[s * N:(s + 1) * N, :N] for s in range(S)], axis=1),
             jnp.concatenate([y[s * N:(s + 1) * N, N:] for s in range(S)], axis=1)], axis=0)
        yh, yl = split(y)
        mh, ml = mats[left, 0], mats[left, 1]
        z = dot(mh, yh) + (dot(mh, yl) + dot(ml, yh))
        return ([z[:N, s * N:(s + 1) * N] for s in range(S)],
                [z[N:, s * N:(s + 1) * N] for s in range(S)])

    forward_halo(0)
    for k in range(K):
        assemble(k)
        if k + 1 < K:
            forward_halo(k + 1)
        if k == 0:
            fetch_probe.wait()
            for fetch in fetch_mats:
                fetch.wait()
        exit_re, exit_im = [], []
        for s in range(S):
            tr, ti = window(k, s, 0), window(k, s, 1)
            patch[k, s, 0] = tr
            patch[k, s, 1] = ti
            if k == 0:
                wr, wi = probe[0], probe[1]
            else:
                wr, wi = wave[k - 1, s, 0], wave[k - 1, s, 1]
            exit_re.append(wr * tr - wi * ti)
            exit_im.append(wr * ti + wi * tr)
        if k + 1 < K:
            next_re, next_im = sandwich(exit_re, exit_im, 0, 1)
            for s in range(S):
                wave[k, s, 0] = next_re[s]
                wave[k, s, 1] = next_im[s]
        else:
            far_re, far_im = sandwich(exit_re, exit_im, 2, 3)

    fetch_meas.wait()
    grad_re, grad_im = [], []
    for s in range(S):
        amplitude = jnp.sqrt(far_re[s] * far_re[s] + far_im[s] * far_im[s] + 1.0)
        factor = (2.0 * live[s]) * (amplitude - meas[0, 0, s]) / amplitude
        grad_re.append(factor * far_re[s])
        grad_im.append(factor * far_im[s])

    def fold_columns(k):
        receive("gcol", k)
        left, right = g_in[k, 0], g_in[k, 1]
        mask = jnp.concatenate([low, low], axis=0)
        add_re = jnp.where(mask, left, turn(right))
        add_im = jnp.where(mask, turn(left), right)
        for p, add in ((0, add_re), (1, add_im)):
            total = padded[k, p, 0] + add
            m_send[k, 0, p] = total[:H]
            m_send[k, 1, p] = total[H + N:]
            out[k, p] = total[H:H + N]
        send("grow", k)

    for k in range(K - 1, -1, -1):
        right, left = (3, 2) if k == K - 1 else (1, 0)
        ge_re, ge_im = sandwich(grad_re, grad_im, right, left)
        for s in range(S):
            if k == 0:
                wr, wi = probe[0], probe[1]
            else:
                wr, wi = wave[k - 1, s, 0], wave[k - 1, s, 1]
            parts = (wr * ge_re[s] + wi * ge_im[s], wr * ge_im[s] - wi * ge_re[s])
            for p in range(2):
                moved = pltpu.roll(parts[p], xs[s], 1)
                zpad[s, p, 0, pl.ds(N, N), :] = jnp.where(lane >= xs[s], moved, 0.0)
                zpad[s, p, 1, pl.ds(N, N), :] = jnp.where(lane < xs[s], moved, 0.0)
        halves = []
        for p in range(2):
            halves.append([sum(zpad[s, p, h, pl.ds(N - ys[s], 2 * N), :] for s in range(S))
                           for h in range(2)])
        (re_lo, re_hi), (im_lo, im_hi) = halves
        mask = jnp.concatenate([low, low], axis=0)
        g_send[k, 0] = jnp.where(mask, re_lo, turn(im_lo))
        g_send[k, 1] = jnp.where(mask, turn(re_hi), im_hi)
        send("gcol", k)
        padded[k, 0, 0] = turn(jnp.where(mask, re_hi, re_lo))
        padded[k, 1, 0] = turn(jnp.where(mask, im_hi, im_lo))
        new_re, new_im = [], []
        for s in range(S):
            tr, ti = patch[k, s, 0], patch[k, s, 1]
            new_re.append(tr * ge_re[s] + ti * ge_im[s])
            new_im.append(tr * ge_im[s] - ti * ge_re[s])
        grad_re, grad_im = new_re, new_im
        if k + 1 < K:
            fold_columns(k + 1)

    pg[pl.ds(0, N), :] = sum(grad_re)
    pg[pl.ds(N, N), :] = sum(grad_im)
    h1 = 2 * N // C
    owners = min(R, h1 // 8)
    h2 = h1 // owners

    def piece(index, size):
        return pl.ds(pl.multiple_of(index * size, 8), size)

    def exchange(me, peer, src, dst, send_sem, recv_sem, device):
        return pltpu.make_async_remote_copy(
            src_ref=src, dst_ref=dst, send_sem=send_sem.at[peer], recv_sem=recv_sem.at[me],
            device_id=device, device_id_type=MESH)

    def col_scatter(me, peer):
        return exchange(me, peer, pg.at[piece(peer, h1)], s1.at[me], as_sem.at[0], ar_sem.at[0], (r, peer))

    def row_scatter(me, peer):
        return exchange(me, peer, q1.at[piece(peer, h2)], s2.at[me], bs_sem.at[0], br_sem.at[0], (peer, c))

    def row_gather(me, peer):
        return exchange(me, peer, q2, f2.at[piece(me, h2)], bs_sem.at[1], br_sem.at[1], (peer, c))

    def col_gather(me, peer):
        return exchange(me, peer, f2, pg_out.at[piece(me, h1)], as_sem.at[1], ar_sem.at[1], (r, peer))

    def when_owner(index, action):
        if owners == R:
            action()
        else:
            pl.when(index < owners)(action)

    col_peers = [lax.rem(c + j, C) for j in range(1, C)]
    row_peers = [lax.rem(r + j, R) for j in range(1, R)]

    for peer in col_peers:
        col_scatter(c, peer).start()
    fold_columns(0)
    s1[c] = pg[piece(c, h1), :]
    for peer in col_peers:
        col_scatter(peer, c).wait_recv()
    q1[...] = sum(s1[j] for j in range(C))
    for peer in row_peers:
        when_owner(peer, lambda: row_scatter(r, peer).start())

    def reduce_rows():
        s2[r] = q1[piece(r, h2), :]
        for peer in row_peers:
            row_scatter(peer, r).wait_recv()
        total = sum(s2[j] for j in range(R))
        q2[...] = total
        f2[piece(r, h2), :] = total
        for peer in row_peers:
            row_gather(r, peer).start()

    when_owner(r, reduce_rows)
    for peer in row_peers:
        when_owner(peer, lambda: row_gather(peer, r).wait_recv())
    for peer in col_peers:
        col_gather(c, peer).start()
    pg_out[piece(c, h1), :] = f2[...]

    for k in range(K - 1, -1, -1):
        receive("grow", k)
        for p in range(2):
            out[k, p, pl.ds(0, H), :] += m_in[k, 0, p]
            out[k, p, pl.ds(H, H), :] += m_in[k, 1, p]

    for peer in col_peers:
        col_gather(peer, c).wait_recv()
    sent()
    for peer in col_peers:
        col_scatter(c, peer).wait_send()
        col_gather(c, peer).wait_send()
    for peer in row_peers:
        when_owner(peer, lambda: row_scatter(r, peer).wait_send())
    for peer in row_peers:
        when_owner(r, lambda: row_gather(r, peer).wait_send())


def per_device(R, C, object_field, probe_wave, positions, counts, measured):
    K, _, N, _ = object_field.shape
    S = measured.shape[2]
    H = N // 2
    f32 = jnp.float32
    h1 = 2 * N // C
    owners = min(R, h1 // 8)
    h2 = h1 // owners
    vmem = pl.BlockSpec(memory_space=pltpu.VMEM)
    hbm = pl.BlockSpec(memory_space=pltpu.HBM)
    smem = pl.BlockSpec(memory_space=pltpu.SMEM)
    dma = pltpu.SemaphoreType.DMA
    grad, probe_grad = pl.pallas_call(
        functools.partial(kernel, R, C),
        out_shape=(jax.ShapeDtypeStruct(object_field.shape, f32), jax.ShapeDtypeStruct((2 * N, N), f32)),
        in_specs=[smem, smem, hbm, hbm, hbm, hbm],
        out_specs=(vmem, vmem),
        scratch_shapes=[
            pltpu.VMEM(object_field.shape, f32),
            pltpu.VMEM(probe_wave.shape, f32),
            pltpu.VMEM(measured.shape, f32),
            pltpu.VMEM((4, 2, 2 * N, 2 * N), jnp.bfloat16),
            pltpu.VMEM((K, 2, 2, H, N), f32),
            pltpu.VMEM((K, 2, 2, N, N), f32),
            pltpu.VMEM((K, 2, 2, N, N), f32),
            pltpu.VMEM((K, 2, 2, 2 * N, N), f32),
            pltpu.VMEM((K, S, 2, N, N), f32),
            pltpu.VMEM((K - 1, S, 2, N, N), f32),
            pltpu.VMEM((S, 2, 2, 3 * N, N), f32),
            pltpu.VMEM((K, 2, 2 * N, N), f32),
            pltpu.VMEM((K, 2, 2 * N, N), f32),
            pltpu.VMEM((K, 2, 2, H, N), f32),
            pltpu.VMEM((K, 2, 2, H, N), f32),
            pltpu.VMEM((2 * N, N), f32),
            pltpu.VMEM((C, h1, N), f32),
            pltpu.VMEM((h1, N), f32),
            pltpu.VMEM((R, h2, N), f32),
            pltpu.VMEM((h2, N), f32),
            pltpu.VMEM((h1, N), f32),
            dma((5, K, 2)), dma((5, K, 2)),
            dma((2, C)), dma((2, C)),
            dma((2, R)), dma((2, R)),
            dma((K + 6,)),
        ],
        compiler_params=pltpu.CompilerParams(
            collective_id=0, has_side_effects=True, vmem_limit_bytes=40 * 1024 * 1024),
    )(positions, counts, object_field, probe_wave, measured, jnp.asarray(tables(N)))
    return grad, probe_grad.reshape(2, N, N)


def solution(mesh):
    in_specs = (
        P(None, None, "row", "col"),
        P(),
        P("row", "col", None, None),
        P("row", "col"),
        P("row", "col", None, None, None),
    )
    out_specs = (P(None, None, "row", "col"), P())
    body = functools.partial(per_device, mesh.shape["row"], mesh.shape["col"])
    return jax.shard_map(body, mesh=mesh, in_specs=in_specs, out_specs=out_specs, check_vma=False)
```

```python
import functools
import math

import jax
import jax.numpy as jnp
import numpy as np
from jax import lax
from jax.experimental import pallas as pl
from jax.experimental.pallas import tpu as pltpu
from jax.sharding import PartitionSpec as P

FRESNEL = 0.01
MESH = pl.DeviceIdType.MESH


def tables(points):
    index = np.arange(points)
    dft = np.exp(-2j * math.pi * ((index[:, None] * index[None, :]) % points) / points) / math.sqrt(points)
    freq = np.where(index < points // 2, index, index - points).astype(np.float64)
    step = np.conj(dft) @ (np.exp(-1j * FRESNEL * freq**2)[:, None] * dft)
    return np.stack([np.stack([m.real, m.imag]) for m in (step, dft)]).astype(np.float32)


def split(x):
    high = x.astype(jnp.bfloat16)
    return high, (x - high.astype(jnp.float32)).astype(jnp.bfloat16)


def dot(a, b):
    return jnp.dot(a, b, preferred_element_type=jnp.float32)


def kernel(R, C, pos, cnt, obj_h, probe_h, meas_h, tab_h, out_h, pg_h,
           obj, probe, meas, tab, mats, out,
           row_in, col_send, col_in, padded, patch, wave, zpad, g_send, g_in, m_send, m_in,
           pg, s1, q1, s2, q2, f2,
           hs_sem, hr_sem, as_sem, ar_sem, bs_sem, br_sem, local_sem):
    K = obj_h.shape[0]
    N = obj_h.shape[-1]
    H = N // 2
    S = meas.shape[2]
    r = lax.axis_index("row")
    c = lax.axis_index("col")

    barrier = pltpu.get_barrier_semaphore()
    for j in range(1, R):
        pl.semaphore_signal(barrier, inc=1, device_id=(lax.rem(r + j, R), c), device_id_type=MESH)
    for j in range(1, C):
        pl.semaphore_signal(barrier, inc=1, device_id=(r, lax.rem(c + j, C)), device_id_type=MESH)

    fetch_obj = [pltpu.make_async_copy(obj_h.at[k], obj.at[k], local_sem.at[k]) for k in range(K)]
    fetch_probe = pltpu.make_async_copy(probe_h, probe, local_sem.at[K])
    fetch_meas = pltpu.make_async_copy(meas_h, meas, local_sem.at[K + 1])
    fetch_tab = pltpu.make_async_copy(tab_h, tab, local_sem.at[K + 2])
    for fetch in fetch_obj + [fetch_tab, fetch_probe, fetch_meas]:
        fetch.start()

    have = {"up": r > 0, "down": r < R - 1, "left": c > 0, "right": c < C - 1}
    where_to = {"up": (r - 1, c), "down": (r + 1, c), "left": (r, c - 1), "right": (r, c + 1)}
    back = {"up": "down", "down": "up", "left": "right", "right": "left"}
    slot = {"up": 0, "down": 1, "left": 0, "right": 1}

    def row_refs(k, side):
        rows = pl.ds(0, H) if side == "up" else pl.ds(H, H)
        return obj_h.at[k, :, rows, :], row_in.at[k, slot[back[side]]]

    def own_refs(k, side):
        return col_send.at[k, slot[side], 0], col_in.at[k, slot[back[side]], 0]

    def halo_refs(k, side):
        return col_send.at[k, slot[side], 1], col_in.at[k, slot[back[side]], 1]

    def gcol_refs(k, side):
        return g_send.at[k, slot[side]], g_in.at[k, slot[back[side]]]

    def grow_refs(k, side):
        return m_send.at[k, slot[side]], m_in.at[k, slot[back[side]]]

    kinds = {"row": (0, row_refs, ("up", "down")), "own": (1, own_refs, ("left", "right")),
             "halo": (2, halo_refs, ("left", "right")), "gcol": (3, gcol_refs, ("left", "right")),
             "grow": (4, grow_refs, ("up", "down"))}

    def copy_to(kind, k, side):
        number, refs, _ = kinds[kind]
        src, dst = refs(k, side)
        return pltpu.make_async_remote_copy(
            src_ref=src, dst_ref=dst,
            send_sem=hs_sem.at[number, k, slot[side]],
            recv_sem=hr_sem.at[number, k, slot[back[side]]],
            device_id=where_to[side], device_id_type=MESH)

    def send(kind, k):
        for side in kinds[kind][2]:
            @pl.when(have[side])
            def _():
                copy_to(kind, k, side).start()

    def receive(kind, k):
        for side in kinds[kind][2]:
            @pl.when(have[side])
            def _():
                number, refs, _ = kinds[kind]
                src, dst = refs(k, back[side])
                pltpu.make_async_remote_copy(
                    src_ref=src, dst_ref=dst,
                    send_sem=hs_sem.at[number, k, slot[back[side]]],
                    recv_sem=hr_sem.at[number, k, slot[side]],
                    device_id=where_to[side], device_id_type=MESH).wait_recv()

    def sent():
        for side in have:
            @pl.when(have[side])
            def _():
                for kind in kinds:
                    if side in kinds[kind][2]:
                        for k in range(K):
                            copy_to(kind, k, side).wait_send()

    lane = lax.broadcasted_iota(jnp.int32, (N, N), 1)
    low = lane < H
    low_h = lane[:H] < H

    def turn(x):
        return pltpu.roll(x, H, 1)

    for side, buffers in (("up", (row_in, m_in)), ("down", (row_in, m_in)),
                          ("left", (col_in, g_in)), ("right", (col_in, g_in))):
        @pl.when(jnp.logical_not(have[side]))
        def _():
            for buffer in buffers:
                for k in range(K):
                    buffer[k, slot[side]] = jnp.zeros(buffer.shape[2:], jnp.float32)
    for s in range(S):
        for p in range(2):
            zpad[s, p, :, pl.ds(0, N), :] = jnp.zeros((2, N, N), jnp.float32)
            zpad[s, p, :, pl.ds(2 * N, N), :] = jnp.zeros((2, N, N), jnp.float32)

    fetch_tab.wait()
    for i in range(2):
        for part, (re, im) in enumerate(zip(split(tab[i, 0]), split(tab[i, 1]))):
            for form, (upper, lower) in enumerate(((im, -im), (-im, im))):
                mats[2 * i + form, part, pl.ds(0, N), pl.ds(0, N)] = re
                mats[2 * i + form, part, pl.ds(0, N), pl.ds(N, N)] = upper
                mats[2 * i + form, part, pl.ds(N, N), pl.ds(0, N)] = lower
                mats[2 * i + form, part, pl.ds(N, N), pl.ds(N, N)] = re
    pl.semaphore_wait(barrier, R + C - 2)

    def pack_own(k):
        fetch_obj[k].wait()
        re, im = obj[k, 0], obj[k, 1]
        col_send[k, 0, 0] = jnp.where(low, re, turn(im))
        col_send[k, 1, 0] = jnp.where(low, turn(re), im)
        send("own", k)

    send("row", 0)
    pack_own(0)
    send("row", 1)
    pack_own(1)

    ys = [jnp.clip(pos[0, 0, s, 0] - r * N, 0, N - 1) for s in range(S)]
    xs = [jnp.clip(pos[0, 0, s, 1] - c * N, 0, N - 1) for s in range(S)]
    live = [(s < cnt[0, 0]).astype(jnp.float32) for s in range(S)]

    def forward_halo(k):
        receive("row", k)
        for d in range(2):
            re, im = row_in[k, d, 0], row_in[k, d, 1]
            rows = pl.ds(d * H, H)
            col_send[k, 0, 1, rows, :] = jnp.where(low_h, re, turn(im))
            col_send[k, 1, 1, rows, :] = jnp.where(low_h, turn(re), im)
        send("halo", k)
        if k + 2 < K:
            send("row", k + 2)
            pack_own(k + 2)

    def assemble(k):
        receive("own", k)
        receive("halo", k)
        for start, size, mid, part, begin in (
                (0, H, lambda p: row_in[k, 0, p], 1, 0),
                (H, N, lambda p: obj[k, p], 0, 0),
                (H + N, H, lambda p: row_in[k, 1, p], 1, H)):
            left = col_in[k, 0, part, pl.ds(begin, size), :]
            right = col_in[k, 1, part, pl.ds(begin, size), :]
            mask = low if size == N else low_h
            re, im = mid(0), mid(1)
            rows = pl.ds(start, size)
            padded[k, 0, 0, rows, :] = jnp.where(mask, left, turn(re))
            padded[k, 0, 1, rows, :] = turn(jnp.where(mask, right, re))
            padded[k, 1, 0, rows, :] = turn(jnp.where(mask, im, left))
            padded[k, 1, 1, rows, :] = jnp.where(mask, turn(im), right)

    def window(k, s, p):
        rows = pl.ds(ys[s], N)
        shift = lax.rem(N - xs[s], N)
        first = pltpu.roll(padded[k, p, 0, rows, :], shift, 1)
        second = pltpu.roll(padded[k, p, 1, rows, :], shift, 1)
        return jnp.where(lane < N - xs[s], first, second)

    def sandwich(res, ims, right, left):
        x = jnp.concatenate([jnp.concatenate([a, b], axis=1) for a, b in zip(res, ims)], axis=0)
        xh, xl = split(x)
        mh, ml = mats[right, 0], mats[right, 1]
        y = dot(jnp.concatenate([xh, xl, xh], axis=1), jnp.concatenate([mh, mh, ml], axis=0))
        y = jnp.concatenate(
            [jnp.concatenate([y[s * N:(s + 1) * N, :N] for s in range(S)], axis=1),
             jnp.concatenate([y[s * N:(s + 1) * N, N:] for s in range(S)], axis=1)], axis=0)
        yh, yl = split(y)
        mh, ml = mats[left, 0], mats[left, 1]
        z = dot(jnp.concatenate([mh, mh, ml], axis=1), jnp.concatenate([yh, yl, yh], axis=0))
        return ([z[:N, s * N:(s + 1) * N] for s in range(S)],
                [z[N:, s * N:(s + 1) * N] for s in range(S)])

    forward_halo(0)
    for k in range(K):
        assemble(k)
        if k + 1 < K:
            forward_halo(k + 1)
        if k == 0:
            fetch_probe.wait()
        exit_re, exit_im = [], []
        for s in range(S):
            tr, ti = window(k, s, 0), window(k, s, 1)
            patch[k, s, 0] = tr
            patch[k, s, 1] = ti
            if k == 0:
                wr, wi = probe[0], probe[1]
            else:
                wr, wi = wave[k - 1, s, 0], wave[k - 1, s, 1]
            exit_re.append(wr * tr - wi * ti)
            exit_im.append(wr * ti + wi * tr)
        if k + 1 < K:
            next_re, next_im = sandwich(exit_re, exit_im, 0, 1)
            for s in range(S):
                wave[k, s, 0] = next_re[s]
                wave[k, s, 1] = next_im[s]
        else:
            far_re, far_im = sandwich(exit_re, exit_im, 2, 3)

    fetch_meas.wait()
    grad_re, grad_im = [], []
    for s in range(S):
        amplitude = jnp.sqrt(far_re[s] * far_re[s] + far_im[s] * far_im[s] + 1.0)
        factor = (2.0 * live[s]) * (amplitude - meas[0, 0, s]) / amplitude
        grad_re.append(factor * far_re[s])
        grad_im.append(factor * far_im[s])

    def fold_columns(k):
        receive("gcol", k)
        left, right = g_in[k, 0], g_in[k, 1]
        mask = jnp.concatenate([low, low], axis=0)
        add_re = jnp.where(mask, left, turn(right))
        add_im = jnp.where(mask, turn(left), right)
        for p, add in ((0, add_re), (1, add_im)):
            total = padded[k, p, 0] + add
            m_send[k, 0, p] = total[:H]
            m_send[k, 1, p] = total[H + N:]
            out[k, p] = total[H:H + N]
        send("grow", k)

    for k in range(K - 1, -1, -1):
        right, left = (3, 2) if k == K - 1 else (1, 0)
        ge_re, ge_im = sandwich(grad_re, grad_im, right, left)
        for s in range(S):
            if k == 0:
                wr, wi = probe[0], probe[1]
            else:
                wr, wi = wave[k - 1, s, 0], wave[k - 1, s, 1]
            parts = (wr * ge_re[s] + wi * ge_im[s], wr * ge_im[s] - wi * ge_re[s])
            for p in range(2):
                moved = pltpu.roll(parts[p], xs[s], 1)
                zpad[s, p, 0, pl.ds(N, N), :] = jnp.where(lane >= xs[s], moved, 0.0)
                zpad[s, p, 1, pl.ds(N, N), :] = jnp.where(lane < xs[s], moved, 0.0)
        halves = []
        for p in range(2):
            halves.append([sum(zpad[s, p, h, pl.ds(N - ys[s], 2 * N), :] for s in range(S))
                           for h in range(2)])
        (re_lo, re_hi), (im_lo, im_hi) = halves
        mask = jnp.concatenate([low, low], axis=0)
        g_send[k, 0] = jnp.where(mask, re_lo, turn(im_lo))
        g_send[k, 1] = jnp.where(mask, turn(re_hi), im_hi)
        send("gcol", k)
        padded[k, 0, 0] = turn(jnp.where(mask, re_hi, re_lo))
        padded[k, 1, 0] = turn(jnp.where(mask, im_hi, im_lo))
        new_re, new_im = [], []
        for s in range(S):
            tr, ti = patch[k, s, 0], patch[k, s, 1]
            new_re.append(tr * ge_re[s] + ti * ge_im[s])
            new_im.append(tr * ge_im[s] - ti * ge_re[s])
        grad_re, grad_im = new_re, new_im
        if k + 1 < K:
            fold_columns(k + 1)

    pg[pl.ds(0, N), :] = sum(grad_re)
    pg[pl.ds(N, N), :] = sum(grad_im)
    h1 = 2 * N // C
    owners = min(R, h1 // 8)
    h2 = h1 // owners

    def piece(index, size):
        return pl.ds(pl.multiple_of(index * size, 8), size)

    def exchange(me, peer, src, dst, send_sem, recv_sem, device):
        return pltpu.make_async_remote_copy(
            src_ref=src, dst_ref=dst, send_sem=send_sem.at[peer], recv_sem=recv_sem.at[me],
            device_id=device, device_id_type=MESH)

    def col_scatter(me, peer):
        return exchange(me, peer, pg.at[piece(peer, h1)], s1.at[me], as_sem.at[0], ar_sem.at[0], (r, peer))

    def row_scatter(me, peer):
        return exchange(me, peer, q1.at[piece(peer, h2)], s2.at[me], bs_sem.at[0], br_sem.at[0], (peer, c))

    def row_gather(me, peer):
        return exchange(me, peer, q2, f2.at[piece(me, h2)], bs_sem.at[1], br_sem.at[1], (peer, c))

    def pg_piece(me):
        return pg_h.at[(me * h1) // N, piece(lax.rem(me, N // h1), h1)]

    def col_gather(me, peer):
        return exchange(me, peer, f2, pg_piece(me), as_sem.at[1], ar_sem.at[1], (r, peer))

    def when_owner(index, action):
        if owners == R:
            action()
        else:
            pl.when(index < owners)(action)

    col_peers = [lax.rem(c + j, C) for j in range(1, C)]
    row_peers = [lax.rem(r + j, R) for j in range(1, R)]

    for peer in col_peers:
        col_scatter(c, peer).start()
    fold_columns(0)
    s1[c] = pg[piece(c, h1), :]
    for peer in col_peers:
        col_scatter(peer, c).wait_recv()
    q1[...] = sum(s1[j] for j in range(C))
    for peer in row_peers:
        when_owner(peer, lambda: row_scatter(r, peer).start())

    def reduce_rows():
        s2[r] = q1[piece(r, h2), :]
        for peer in row_peers:
            row_scatter(peer, r).wait_recv()
        total = sum(s2[j] for j in range(R))
        q2[...] = total
        f2[piece(r, h2), :] = total
        for peer in row_peers:
            row_gather(r, peer).start()

    when_owner(r, reduce_rows)
    for peer in row_peers:
        when_owner(peer, lambda: row_gather(peer, r).wait_recv())
    for peer in col_peers:
        col_gather(c, peer).start()
    keep = pltpu.make_async_copy(f2, pg_piece(c), local_sem.at[K + 3])
    keep.start()

    store_out = [pltpu.make_async_copy(out.at[k], out_h.at[k], local_sem.at[K + 4 + k]) for k in range(K)]
    for k in range(K - 1, -1, -1):
        receive("grow", k)
        for p in range(2):
            out[k, p, pl.ds(0, H), :] += m_in[k, 0, p]
            out[k, p, pl.ds(H, H), :] += m_in[k, 1, p]
        store_out[k].start()

    for peer in col_peers:
        col_gather(peer, c).wait_recv()
    sent()
    for peer in col_peers:
        col_scatter(c, peer).wait_send()
        col_gather(c, peer).wait_send()
    for peer in row_peers:
        when_owner(peer, lambda: row_scatter(r, peer).wait_send())
    for peer in row_peers:
        when_owner(r, lambda: row_gather(r, peer).wait_send())
    for store in [keep] + store_out:
        store.wait()


def per_device(R, C, object_field, probe_wave, positions, counts, measured):
    K, _, N, _ = object_field.shape
    S = measured.shape[2]
    H = N // 2
    f32 = jnp.float32
    h1 = 2 * N // C
    owners = min(R, h1 // 8)
    h2 = h1 // owners
    hbm = pl.BlockSpec(memory_space=pltpu.HBM)
    smem = pl.BlockSpec(memory_space=pltpu.SMEM)
    dma = pltpu.SemaphoreType.DMA
    grad, probe_grad = pl.pallas_call(
        functools.partial(kernel, R, C),
        out_shape=(jax.ShapeDtypeStruct(object_field.shape, f32), jax.ShapeDtypeStruct(probe_wave.shape, f32)),
        in_specs=[smem, smem, hbm, hbm, hbm, hbm],
        out_specs=(hbm, hbm),
        scratch_shapes=[
            pltpu.VMEM(object_field.shape, f32),
            pltpu.VMEM(probe_wave.shape, f32),
            pltpu.VMEM(measured.shape, f32),
            pltpu.VMEM((2, 2, N, N), f32),
            pltpu.VMEM((4, 2, 2 * N, 2 * N), jnp.bfloat16),
            pltpu.VMEM(object_field.shape, f32),
            pltpu.VMEM((K, 2, 2, H, N), f32),
            pltpu.VMEM((K, 2, 2, N, N), f32),
            pltpu.VMEM((K, 2, 2, N, N), f32),
            pltpu.VMEM((K, 2, 2, 2 * N, N), f32),
            pltpu.VMEM((K, S, 2, N, N), f32),
            pltpu.VMEM((K - 1, S, 2, N, N), f32),
            pltpu.VMEM((S, 2, 2, 3 * N, N), f32),
            pltpu.VMEM((K, 2, 2 * N, N), f32),
            pltpu.VMEM((K, 2, 2 * N, N), f32),
            pltpu.VMEM((K, 2, 2, H, N), f32),
            pltpu.VMEM((K, 2, 2, H, N), f32),
            pltpu.VMEM((2 * N, N), f32),
            pltpu.VMEM((C, h1, N), f32),
            pltpu.VMEM((h1, N), f32),
            pltpu.VMEM((R, h2, N), f32),
            pltpu.VMEM((h2, N), f32),
            pltpu.VMEM((h1, N), f32),
            dma((5, K, 2)), dma((5, K, 2)),
            dma((2, C)), dma((2, C)),
            dma((2, R)), dma((2, R)),
            dma((2 * K + 4,)),
        ],
        compiler_params=pltpu.CompilerParams(
            collective_id=0, has_side_effects=True, vmem_limit_bytes=63 * 1024 * 1024),
    )(positions, counts, object_field, probe_wave, measured, jnp.asarray(tables(N)))
    return grad, probe_grad


def solution(mesh):
    in_specs = (
        P(None, None, "row", "col"),
        P(),
        P("row", "col", None, None),
        P("row", "col"),
        P("row", "col", None, None, None),
    )
    out_specs = (P(None, None, "row", "col"), P())
    body = functools.partial(per_device, mesh.shape["row"], mesh.shape["col"])
    return jax.shard_map(body, mesh=mesh, in_specs=in_specs, out_specs=out_specs, check_vma=False)
```

```python
import functools
import math

import jax
import jax.numpy as jnp
import numpy as np
from jax import lax
from jax.experimental import pallas as pl
from jax.experimental.pallas import tpu as pltpu
from jax.sharding import PartitionSpec as P

FRESNEL = 0.01
MESH = pl.DeviceIdType.MESH


def tables(points):
    index = np.arange(points)
    dft = np.exp(-2j * math.pi * ((index[:, None] * index[None, :]) % points) / points) / math.sqrt(points)
    freq = np.where(index < points // 2, index, index - points).astype(np.float64)
    step = np.conj(dft) @ (np.exp(-1j * FRESNEL * freq**2)[:, None] * dft)
    return np.stack([np.stack([m.real, m.imag]) for m in (step, dft)]).astype(np.float32)


def split(x):
    high = x.astype(jnp.bfloat16)
    return high, (x - high.astype(jnp.float32)).astype(jnp.bfloat16)


def dot(a, b):
    return jnp.dot(a, b, preferred_element_type=jnp.float32)


def kernel(R, C, pos, cnt, obj_h, probe_h, meas_h, tab_h, out_h, pg_h,
           obj, probe, meas, tab, mats, out,
           row_in, col_send, col_in, padded, patch, wave, zpad, g_send, g_in, m_send, m_in,
           pg, s1, q1, s2, q2, f2,
           hs_sem, hr_sem, as_sem, ar_sem, bs_sem, br_sem, local_sem):
    K = obj_h.shape[0]
    N = obj_h.shape[-1]
    H = N // 2
    S = meas.shape[2]
    r = lax.axis_index("row")
    c = lax.axis_index("col")

    barrier = pltpu.get_barrier_semaphore()
    for j in range(1, R):
        pl.semaphore_signal(barrier, inc=1, device_id=(lax.rem(r + j, R), c), device_id_type=MESH)
    for j in range(1, C):
        pl.semaphore_signal(barrier, inc=1, device_id=(r, lax.rem(c + j, C)), device_id_type=MESH)

    fetch_obj = [pltpu.make_async_copy(obj_h.at[k], obj.at[k], local_sem.at[k]) for k in range(K)]
    fetch_probe = pltpu.make_async_copy(probe_h, probe, local_sem.at[K])
    fetch_meas = pltpu.make_async_copy(meas_h, meas, local_sem.at[K + 1])
    fetch_tab = pltpu.make_async_copy(tab_h, tab, local_sem.at[K + 2])
    for fetch in fetch_obj + [fetch_tab, fetch_probe, fetch_meas]:
        fetch.start()

    have = {"up": r > 0, "down": r < R - 1, "left": c > 0, "right": c < C - 1}
    where_to = {"up": (r - 1, c), "down": (r + 1, c), "left": (r, c - 1), "right": (r, c + 1)}
    back = {"up": "down", "down": "up", "left": "right", "right": "left"}
    slot = {"up": 0, "down": 1, "left": 0, "right": 1}

    def row_refs(k, side):
        rows = pl.ds(0, H) if side == "up" else pl.ds(H, H)
        return obj_h.at[k, :, rows, :], row_in.at[k, slot[back[side]]]

    def own_refs(k, side):
        return col_send.at[k, slot[side], 0], col_in.at[k, slot[back[side]], 0]

    def halo_refs(k, side):
        return col_send.at[k, slot[side], 1], col_in.at[k, slot[back[side]], 1]

    def gcol_refs(k, side):
        return g_send.at[k, slot[side]], g_in.at[k, slot[back[side]]]

    def grow_refs(k, side):
        return m_send.at[k, slot[side]], m_in.at[k, slot[back[side]]]

    kinds = {"row": (0, row_refs, ("up", "down")), "own": (1, own_refs, ("left", "right")),
             "halo": (2, halo_refs, ("left", "right")), "gcol": (3, gcol_refs, ("left", "right")),
             "grow": (4, grow_refs, ("up", "down"))}

    def copy_to(kind, k, side):
        number, refs, _ = kinds[kind]
        src, dst = refs(k, side)
        return pltpu.make_async_remote_copy(
            src_ref=src, dst_ref=dst,
            send_sem=hs_sem.at[number, k, slot[side]],
            recv_sem=hr_sem.at[number, k, slot[back[side]]],
            device_id=where_to[side], device_id_type=MESH)

    def send(kind, k):
        for side in kinds[kind][2]:
            @pl.when(have[side])
            def _():
                copy_to(kind, k, side).start()

    def receive(kind, k):
        for side in kinds[kind][2]:
            @pl.when(have[side])
            def _():
                number, refs, _ = kinds[kind]
                src, dst = refs(k, back[side])
                pltpu.make_async_remote_copy(
                    src_ref=src, dst_ref=dst,
                    send_sem=hs_sem.at[number, k, slot[back[side]]],
                    recv_sem=hr_sem.at[number, k, slot[side]],
                    device_id=where_to[side], device_id_type=MESH).wait_recv()

    def sent():
        for side in have:
            @pl.when(have[side])
            def _():
                for kind in kinds:
                    if side in kinds[kind][2]:
                        for k in range(K):
                            copy_to(kind, k, side).wait_send()

    lane = lax.broadcasted_iota(jnp.int32, (N, N), 1)
    low = lane < H
    low_h = lane[:H] < H

    def turn(x):
        return pltpu.roll(x, H, 1)

    pl.semaphore_wait(barrier, R + C - 2)
    send("row", 0)

    def pack_own(k):
        fetch_obj[k].wait()
        re, im = obj[k, 0], obj[k, 1]
        col_send[k, 0, 0] = jnp.where(low, re, turn(im))
        col_send[k, 1, 0] = jnp.where(low, turn(re), im)
        send("own", k)

    pack_own(0)
    send("row", 1)
    for side, buffers in (("up", (row_in, m_in)), ("down", (row_in, m_in)),
                          ("left", (col_in, g_in)), ("right", (col_in, g_in))):
        @pl.when(jnp.logical_not(have[side]))
        def _():
            for buffer in buffers:
                for k in range(K):
                    buffer[k, slot[side]] = jnp.zeros(buffer.shape[2:], jnp.float32)
    for s in range(S):
        for p in range(2):
            zpad[s, p, :, pl.ds(0, N), :] = jnp.zeros((2, N, N), jnp.float32)
            zpad[s, p, :, pl.ds(2 * N, N), :] = jnp.zeros((2, N, N), jnp.float32)

    fetch_tab.wait()
    for i in range(2):
        for part, (re, im) in enumerate(zip(split(tab[i, 0]), split(tab[i, 1]))):
            for form, (upper, lower) in enumerate(((im, -im), (-im, im))):
                mats[2 * i + form, part, pl.ds(0, N), pl.ds(0, N)] = re
                mats[2 * i + form, part, pl.ds(0, N), pl.ds(N, N)] = upper
                mats[2 * i + form, part, pl.ds(N, N), pl.ds(0, N)] = lower
                mats[2 * i + form, part, pl.ds(N, N), pl.ds(N, N)] = re
    pack_own(1)

    ys = [jnp.clip(pos[0, 0, s, 0] - r * N, 0, N - 1) for s in range(S)]
    xs = [jnp.clip(pos[0, 0, s, 1] - c * N, 0, N - 1) for s in range(S)]
    live = [(s < cnt[0, 0]).astype(jnp.float32) for s in range(S)]

    def forward_halo(k):
        receive("row", k)
        for d in range(2):
            re, im = row_in[k, d, 0], row_in[k, d, 1]
            rows = pl.ds(d * H, H)
            col_send[k, 0, 1, rows, :] = jnp.where(low_h, re, turn(im))
            col_send[k, 1, 1, rows, :] = jnp.where(low_h, turn(re), im)
        send("halo", k)
        if k + 2 < K:
            send("row", k + 2)
            pack_own(k + 2)

    def assemble(k):
        receive("own", k)
        receive("halo", k)
        for start, size, mid, part, begin in (
                (0, H, lambda p: row_in[k, 0, p], 1, 0),
                (H, N, lambda p: obj[k, p], 0, 0),
                (H + N, H, lambda p: row_in[k, 1, p], 1, H)):
            left = col_in[k, 0, part, pl.ds(begin, size), :]
            right = col_in[k, 1, part, pl.ds(begin, size), :]
            mask = low if size == N else low_h
            re, im = mid(0), mid(1)
            rows = pl.ds(start, size)
            padded[k, 0, 0, rows, :] = jnp.where(mask, left, turn(re))
            padded[k, 0, 1, rows, :] = turn(jnp.where(mask, right, re))
            padded[k, 1, 0, rows, :] = turn(jnp.where(mask, im, left))
            padded[k, 1, 1, rows, :] = jnp.where(mask, turn(im), right)

    def window(k, s, p):
        rows = pl.ds(ys[s], N)
        shift = lax.rem(N - xs[s], N)
        first = pltpu.roll(padded[k, p, 0, rows, :], shift, 1)
        second = pltpu.roll(padded[k, p, 1, rows, :], shift, 1)
        return jnp.where(lane < N - xs[s], first, second)

    def sandwich(res, ims, right, left):
        x = jnp.concatenate([jnp.concatenate([a, b], axis=1) for a, b in zip(res, ims)], axis=0)
        xh, xl = split(x)
        mh, ml = mats[right, 0], mats[right, 1]
        y = dot(jnp.concatenate([xh, xl, xh], axis=1), jnp.concatenate([mh, mh, ml], axis=0))
        y = jnp.concatenate(
            [jnp.concatenate([y[s * N:(s + 1) * N, :N] for s in range(S)], axis=1),
             jnp.concatenate([y[s * N:(s + 1) * N, N:] for s in range(S)], axis=1)], axis=0)
        yh, yl = split(y)
        mh, ml = mats[left, 0], mats[left, 1]
        z = dot(jnp.concatenate([mh, mh, ml], axis=1), jnp.concatenate([yh, yl, yh], axis=0))
        return ([z[:N, s * N:(s + 1) * N] for s in range(S)],
                [z[N:, s * N:(s + 1) * N] for s in range(S)])

    forward_halo(0)
    for k in range(K):
        assemble(k)
        if k + 1 < K:
            forward_halo(k + 1)
        if k == 0:
            fetch_probe.wait()
        exit_re, exit_im = [], []
        for s in range(S):
            tr, ti = window(k, s, 0), window(k, s, 1)
            patch[k, s, 0] = tr
            patch[k, s, 1] = ti
            if k == 0:
                wr, wi = probe[0], probe[1]
            else:
                wr, wi = wave[k - 1, s, 0], wave[k - 1, s, 1]
            exit_re.append(wr * tr - wi * ti)
            exit_im.append(wr * ti + wi * tr)
        if k + 1 < K:
            next_re, next_im = sandwich(exit_re, exit_im, 0, 1)
            for s in range(S):
                wave[k, s, 0] = next_re[s]
                wave[k, s, 1] = next_im[s]
        else:
            far_re, far_im = sandwich(exit_re, exit_im, 2, 3)

    fetch_meas.wait()
    grad_re, grad_im = [], []
    for s in range(S):
        amplitude = jnp.sqrt(far_re[s] * far_re[s] + far_im[s] * far_im[s] + 1.0)
        factor = (2.0 * live[s]) * (amplitude - meas[0, 0, s]) / amplitude
        grad_re.append(factor * far_re[s])
        grad_im.append(factor * far_im[s])

    def fold_columns(k):
        receive("gcol", k)
        left, right = g_in[k, 0], g_in[k, 1]
        mask = jnp.concatenate([low, low], axis=0)
        add_re = jnp.where(mask, left, turn(right))
        add_im = jnp.where(mask, turn(left), right)
        for p, add in ((0, add_re), (1, add_im)):
            total = padded[k, p, 0] + add
            m_send[k, 0, p] = total[:H]
            m_send[k, 1, p] = total[H + N:]
            out[k, p] = total[H:H + N]
        send("grow", k)

    h1 = 2 * N // C
    owners = min(R, h1 // 8)
    h2 = h1 // owners

    def piece(index, size):
        return pl.ds(pl.multiple_of(index * size, 8), size)

    def exchange(me, peer, src, dst, send_sem, recv_sem, device):
        return pltpu.make_async_remote_copy(
            src_ref=src, dst_ref=dst, send_sem=send_sem.at[peer], recv_sem=recv_sem.at[me],
            device_id=device, device_id_type=MESH)

    def col_scatter(me, peer):
        return exchange(me, peer, pg.at[piece(peer, h1)], s1.at[me], as_sem.at[0], ar_sem.at[0], (r, peer))

    def row_scatter(me, peer):
        return exchange(me, peer, q1.at[piece(peer, h2)], s2.at[me], bs_sem.at[0], br_sem.at[0], (peer, c))

    def row_gather(me, peer):
        return exchange(me, peer, q2, f2.at[piece(me, h2)], bs_sem.at[1], br_sem.at[1], (peer, c))

    def pg_piece(me):
        return pg_h.at[(me * h1) // N, piece(lax.rem(me, N // h1), h1)]

    def col_gather(me, peer):
        return exchange(me, peer, f2, pg_piece(me), as_sem.at[1], ar_sem.at[1], (r, peer))

    def when_owner(index, action):
        if owners == R:
            action()
        else:
            pl.when(index < owners)(action)

    col_peers = [lax.rem(c + j, C) for j in range(1, C)]
    row_peers = [lax.rem(r + j, R) for j in range(1, R)]

    def start_probe(re, im):
        pg[pl.ds(0, N), :] = sum(re)
        pg[pl.ds(N, N), :] = sum(im)
        for peer in col_peers:
            col_scatter(c, peer).start()

    for k in range(K - 1, -1, -1):
        right, left = (3, 2) if k == K - 1 else (1, 0)
        ge_re, ge_im = sandwich(grad_re, grad_im, right, left)
        new_re, new_im = [], []
        for s in range(S):
            tr, ti = patch[k, s, 0], patch[k, s, 1]
            new_re.append(tr * ge_re[s] + ti * ge_im[s])
            new_im.append(tr * ge_im[s] - ti * ge_re[s])
        grad_re, grad_im = new_re, new_im
        if k == 0:
            start_probe(grad_re, grad_im)
        for s in range(S):
            if k == 0:
                wr, wi = probe[0], probe[1]
            else:
                wr, wi = wave[k - 1, s, 0], wave[k - 1, s, 1]
            parts = (wr * ge_re[s] + wi * ge_im[s], wr * ge_im[s] - wi * ge_re[s])
            for p in range(2):
                moved = pltpu.roll(parts[p], xs[s], 1)
                zpad[s, p, 0, pl.ds(N, N), :] = jnp.where(lane >= xs[s], moved, 0.0)
                zpad[s, p, 1, pl.ds(N, N), :] = jnp.where(lane < xs[s], moved, 0.0)
        halves = []
        for p in range(2):
            halves.append([sum(zpad[s, p, h, pl.ds(N - ys[s], 2 * N), :] for s in range(S))
                           for h in range(2)])
        (re_lo, re_hi), (im_lo, im_hi) = halves
        mask = jnp.concatenate([low, low], axis=0)
        g_send[k, 0] = jnp.where(mask, re_lo, turn(im_lo))
        g_send[k, 1] = jnp.where(mask, turn(re_hi), im_hi)
        send("gcol", k)
        padded[k, 0, 0] = turn(jnp.where(mask, re_hi, re_lo))
        padded[k, 1, 0] = turn(jnp.where(mask, im_hi, im_lo))
        if k + 1 < K:
            fold_columns(k + 1)

    s1[c] = pg[piece(c, h1), :]
    for peer in col_peers:
        col_scatter(peer, c).wait_recv()
    q1[...] = sum(s1[j] for j in range(C))
    for peer in row_peers:
        when_owner(peer, lambda: row_scatter(r, peer).start())
    fold_columns(0)

    def reduce_rows():
        s2[r] = q1[piece(r, h2), :]
        for peer in row_peers:
            row_scatter(peer, r).wait_recv()
        total = sum(s2[j] for j in range(R))
        q2[...] = total
        f2[piece(r, h2), :] = total
        for peer in row_peers:
            row_gather(r, peer).start()

    when_owner(r, reduce_rows)
    for peer in row_peers:
        when_owner(peer, lambda: row_gather(peer, r).wait_recv())
    for peer in col_peers:
        col_gather(c, peer).start()
    keep = pltpu.make_async_copy(f2, pg_piece(c), local_sem.at[K + 3])
    keep.start()

    store_out = [pltpu.make_async_copy(out.at[k], out_h.at[k], local_sem.at[K + 4 + k]) for k in range(K)]
    for k in range(K - 1, -1, -1):
        receive("grow", k)
        for p in range(2):
            out[k, p, pl.ds(0, H), :] += m_in[k, 0, p]
            out[k, p, pl.ds(H, H), :] += m_in[k, 1, p]
        store_out[k].start()

    for peer in col_peers:
        col_gather(peer, c).wait_recv()
    sent()
    for peer in col_peers:
        col_scatter(c, peer).wait_send()
        col_gather(c, peer).wait_send()
    for peer in row_peers:
        when_owner(peer, lambda: row_scatter(r, peer).wait_send())
    for peer in row_peers:
        when_owner(r, lambda: row_gather(r, peer).wait_send())
    for store in [keep] + store_out:
        store.wait()


def copy_kernel(grad, probe_grad, grad_out, probe_out, sems):
    K = grad.shape[0]
    copies = [pltpu.make_async_copy(grad.at[k, p], grad_out.at[k, p], sems.at[2 * k + p])
              for k in range(K) for p in range(2)]
    copies.append(pltpu.make_async_copy(probe_grad, probe_out, sems.at[2 * K]))
    for copy in copies:
        copy.start()
    for copy in copies:
        copy.wait()


def per_device(R, C, object_field, probe_wave, positions, counts, measured):
    K, _, N, _ = object_field.shape
    S = measured.shape[2]
    H = N // 2
    f32 = jnp.float32
    h1 = 2 * N // C
    owners = min(R, h1 // 8)
    h2 = h1 // owners
    hbm = pl.BlockSpec(memory_space=pltpu.HBM)
    smem = pl.BlockSpec(memory_space=pltpu.SMEM)
    dma = pltpu.SemaphoreType.DMA
    grad, probe_grad = pl.pallas_call(
        functools.partial(kernel, R, C),
        out_shape=(jax.ShapeDtypeStruct(object_field.shape, f32), jax.ShapeDtypeStruct(probe_wave.shape, f32)),
        in_specs=[smem, smem, hbm, hbm, hbm, hbm],
        out_specs=(hbm, hbm),
        scratch_shapes=[
            pltpu.VMEM(object_field.shape, f32),
            pltpu.VMEM(probe_wave.shape, f32),
            pltpu.VMEM(measured.shape, f32),
            pltpu.VMEM((2, 2, N, N), f32),
            pltpu.VMEM((4, 2, 2 * N, 2 * N), jnp.bfloat16),
            pltpu.VMEM(object_field.shape, f32),
            pltpu.VMEM((K, 2, 2, H, N), f32),
            pltpu.VMEM((K, 2, 2, N, N), f32),
            pltpu.VMEM((K, 2, 2, N, N), f32),
            pltpu.VMEM((K, 2, 2, 2 * N, N), f32),
            pltpu.VMEM((K, S, 2, N, N), f32),
            pltpu.VMEM((K - 1, S, 2, N, N), f32),
            pltpu.VMEM((S, 2, 2, 3 * N, N), f32),
            pltpu.VMEM((K, 2, 2 * N, N), f32),
            pltpu.VMEM((K, 2, 2 * N, N), f32),
            pltpu.VMEM((K, 2, 2, H, N), f32),
            pltpu.VMEM((K, 2, 2, H, N), f32),
            pltpu.VMEM((2 * N, N), f32),
            pltpu.VMEM((C, h1, N), f32),
            pltpu.VMEM((h1, N), f32),
            pltpu.VMEM((R, h2, N), f32),
            pltpu.VMEM((h2, N), f32),
            pltpu.VMEM((h1, N), f32),
            dma((5, K, 2)), dma((5, K, 2)),
            dma((2, C)), dma((2, C)),
            dma((2, R)), dma((2, R)),
            dma((2 * K + 4,)),
        ],
        compiler_params=pltpu.CompilerParams(
            collective_id=0, has_side_effects=True, vmem_limit_bytes=63 * 1024 * 1024),
    )(positions, counts, object_field, probe_wave, measured, jnp.asarray(tables(N)))
    return pl.pallas_call(
        copy_kernel,
        out_shape=(jax.ShapeDtypeStruct(grad.shape, f32), jax.ShapeDtypeStruct(probe_grad.shape, f32)),
        in_specs=[hbm, hbm],
        out_specs=(hbm, hbm),
        scratch_shapes=[dma((2 * K + 1,))],
        compiler_params=pltpu.CompilerParams(vmem_limit_bytes=63 * 1024 * 1024),
    )(grad, probe_grad)


def solution(mesh):
    in_specs = (
        P(None, None, "row", "col"),
        P(),
        P("row", "col", None, None),
        P("row", "col"),
        P("row", "col", None, None, None),
    )
    out_specs = (P(None, None, "row", "col"), P())
    body = functools.partial(per_device, mesh.shape["row"], mesh.shape["col"])
    return jax.shard_map(body, mesh=mesh, in_specs=in_specs, out_specs=out_specs, check_vma=False)
```

```python
import functools
import math

import jax
import jax.numpy as jnp
import numpy as np
from jax import lax
from jax.experimental import pallas as pl
from jax.experimental.pallas import tpu as pltpu
from jax.sharding import PartitionSpec as P

FRESNEL = 0.01
MESH = pl.DeviceIdType.MESH


def tables(points):
    index = np.arange(points)
    dft = np.exp(-2j * math.pi * ((index[:, None] * index[None, :]) % points) / points) / math.sqrt(points)
    freq = np.where(index < points // 2, index, index - points).astype(np.float64)
    step = np.conj(dft) @ (np.exp(-1j * FRESNEL * freq**2)[:, None] * dft)
    return np.stack([np.stack([m.real, m.imag]) for m in (step, dft)]).astype(np.float32)


def split(x):
    high = x.astype(jnp.bfloat16)
    return high, (x - high.astype(jnp.float32)).astype(jnp.bfloat16)


def dot(a, b):
    return jnp.dot(a, b, preferred_element_type=jnp.float32)


def kernel(R, C, pos, cnt, obj_h, probe_h, meas_h, tab_h, out_h, pg_h,
           obj, probe, meas, tab, mats, out,
           row_in, col_send, col_in, padded, patch, wave, zpad, g_send, g_in, m_send, m_in,
           pg, s1, q1, s2, q2, f2,
           hs_sem, hr_sem, as_sem, ar_sem, bs_sem, br_sem, local_sem):
    K = obj_h.shape[0]
    N = obj_h.shape[-1]
    H = N // 2
    S = meas.shape[2]
    r = lax.axis_index("row")
    c = lax.axis_index("col")

    barrier = pltpu.get_barrier_semaphore()
    for j in range(1, R):
        pl.semaphore_signal(barrier, inc=1, device_id=(lax.rem(r + j, R), c), device_id_type=MESH)
    for j in range(1, C):
        pl.semaphore_signal(barrier, inc=1, device_id=(r, lax.rem(c + j, C)), device_id_type=MESH)

    fetch_obj = [pltpu.make_async_copy(obj_h.at[k], obj.at[k], local_sem.at[k]) for k in range(K)]
    fetch_probe = pltpu.make_async_copy(probe_h, probe, local_sem.at[K])
    fetch_meas = pltpu.make_async_copy(meas_h, meas, local_sem.at[K + 1])
    fetch_tab = pltpu.make_async_copy(tab_h, tab, local_sem.at[K + 2])
    for fetch in fetch_obj + [fetch_tab, fetch_probe, fetch_meas]:
        fetch.start()

    have = {"up": r > 0, "down": r < R - 1, "left": c > 0, "right": c < C - 1}
    where_to = {"up": (r - 1, c), "down": (r + 1, c), "left": (r, c - 1), "right": (r, c + 1)}
    back = {"up": "down", "down": "up", "left": "right", "right": "left"}
    slot = {"up": 0, "down": 1, "left": 0, "right": 1}

    def row_refs(k, side):
        rows = pl.ds(0, H) if side == "up" else pl.ds(H, H)
        return obj_h.at[k, :, rows, :], row_in.at[k, slot[back[side]]]

    def own_refs(k, side):
        return col_send.at[k, slot[side], 0], col_in.at[k, slot[back[side]], 0]

    def halo_refs(k, side):
        return col_send.at[k, slot[side], 1], col_in.at[k, slot[back[side]], 1]

    def gcol_refs(k, side):
        return g_send.at[k, slot[side]], g_in.at[k, slot[back[side]]]

    def grow_refs(k, side):
        return m_send.at[k, slot[side]], m_in.at[k, slot[back[side]]]

    kinds = {"row": (0, row_refs, ("up", "down")), "own": (1, own_refs, ("left", "right")),
             "halo": (2, halo_refs, ("left", "right")), "gcol": (3, gcol_refs, ("left", "right")),
             "grow": (4, grow_refs, ("up", "down"))}

    def copy_to(kind, k, side):
        number, refs, _ = kinds[kind]
        src, dst = refs(k, side)
        return pltpu.make_async_remote_copy(
            src_ref=src, dst_ref=dst,
            send_sem=hs_sem.at[number, k, slot[side]],
            recv_sem=hr_sem.at[number, k, slot[back[side]]],
            device_id=where_to[side], device_id_type=MESH)

    def send(kind, k):
        for side in kinds[kind][2]:
            @pl.when(have[side])
            def _():
                copy_to(kind, k, side).start()

    def receive(kind, k):
        for side in kinds[kind][2]:
            @pl.when(have[side])
            def _():
                number, refs, _ = kinds[kind]
                src, dst = refs(k, back[side])
                pltpu.make_async_remote_copy(
                    src_ref=src, dst_ref=dst,
                    send_sem=hs_sem.at[number, k, slot[back[side]]],
                    recv_sem=hr_sem.at[number, k, slot[side]],
                    device_id=where_to[side], device_id_type=MESH).wait_recv()

    def sent():
        for side in have:
            @pl.when(have[side])
            def _():
                for kind in kinds:
                    if side in kinds[kind][2]:
                        for k in range(K):
                            copy_to(kind, k, side).wait_send()

    lane = lax.broadcasted_iota(jnp.int32, (N, N), 1)
    low = lane < H
    low_h = lane[:H] < H

    def turn(x):
        return pltpu.roll(x, H, 1)

    pl.semaphore_wait(barrier, R + C - 2)
    send("row", 0)

    def pack_own(k):
        fetch_obj[k].wait()
        re, im = obj[k, 0], obj[k, 1]
        col_send[k, 0, 0] = jnp.where(low, re, turn(im))
        col_send[k, 1, 0] = jnp.where(low, turn(re), im)
        send("own", k)

    pack_own(0)
    send("row", 1)
    for side, buffers in (("up", (row_in, m_in)), ("down", (row_in, m_in)),
                          ("left", (col_in, g_in)), ("right", (col_in, g_in))):
        @pl.when(jnp.logical_not(have[side]))
        def _():
            for buffer in buffers:
                for k in range(K):
                    buffer[k, slot[side]] = jnp.zeros(buffer.shape[2:], jnp.float32)
    for s in range(S):
        for p in range(2):
            zpad[s, p, :, pl.ds(0, N), :] = jnp.zeros((2, N, N), jnp.float32)
            zpad[s, p, :, pl.ds(2 * N, N), :] = jnp.zeros((2, N, N), jnp.float32)

    fetch_tab.wait()
    for i in range(2):
        for part, (re, im) in enumerate(zip(split(tab[i, 0]), split(tab[i, 1]))):
            for form, (upper, lower) in enumerate(((im, -im), (-im, im))):
                mats[2 * i + form, part, pl.ds(0, N), pl.ds(0, N)] = re
                mats[2 * i + form, part, pl.ds(0, N), pl.ds(N, N)] = upper
                mats[2 * i + form, part, pl.ds(N, N), pl.ds(0, N)] = lower
                mats[2 * i + form, part, pl.ds(N, N), pl.ds(N, N)] = re
    pack_own(1)

    ys = [jnp.clip(pos[0, 0, s, 0] - r * N, 0, N - 1) for s in range(S)]
    xs = [jnp.clip(pos[0, 0, s, 1] - c * N, 0, N - 1) for s in range(S)]
    live = [(s < cnt[0, 0]).astype(jnp.float32) for s in range(S)]

    def forward_halo(k):
        receive("row", k)
        for d in range(2):
            re, im = row_in[k, d, 0], row_in[k, d, 1]
            rows = pl.ds(d * H, H)
            col_send[k, 0, 1, rows, :] = jnp.where(low_h, re, turn(im))
            col_send[k, 1, 1, rows, :] = jnp.where(low_h, turn(re), im)
        send("halo", k)
        if k + 2 < K:
            send("row", k + 2)
            pack_own(k + 2)

    def assemble(k):
        receive("own", k)
        receive("halo", k)
        for start, size, mid, part, begin in (
                (0, H, lambda p: row_in[k, 0, p], 1, 0),
                (H, N, lambda p: obj[k, p], 0, 0),
                (H + N, H, lambda p: row_in[k, 1, p], 1, H)):
            left = col_in[k, 0, part, pl.ds(begin, size), :]
            right = col_in[k, 1, part, pl.ds(begin, size), :]
            mask = low if size == N else low_h
            re, im = mid(0), mid(1)
            rows = pl.ds(start, size)
            padded[k, 0, 0, rows, :] = jnp.where(mask, left, turn(re))
            padded[k, 0, 1, rows, :] = turn(jnp.where(mask, right, re))
            padded[k, 1, 0, rows, :] = turn(jnp.where(mask, im, left))
            padded[k, 1, 1, rows, :] = jnp.where(mask, turn(im), right)

    def window(k, s, p):
        rows = pl.ds(ys[s], N)
        shift = lax.rem(N - xs[s], N)
        first = pltpu.roll(padded[k, p, 0, rows, :], shift, 1)
        second = pltpu.roll(padded[k, p, 1, rows, :], shift, 1)
        return jnp.where(lane < N - xs[s], first, second)

    def sandwich(res, ims, right, left):
        x = jnp.concatenate([jnp.concatenate([a, b], axis=1) for a, b in zip(res, ims)], axis=0)
        xh, xl = split(x)
        mh, ml = mats[right, 0], mats[right, 1]
        y = dot(jnp.concatenate([xh, xl, xh], axis=1), jnp.concatenate([mh, mh, ml], axis=0))
        y = jnp.concatenate(
            [jnp.concatenate([y[s * N:(s + 1) * N, :N] for s in range(S)], axis=1),
             jnp.concatenate([y[s * N:(s + 1) * N, N:] for s in range(S)], axis=1)], axis=0)
        yh, yl = split(y)
        mh, ml = mats[left, 0], mats[left, 1]
        z = dot(jnp.concatenate([mh, mh, ml], axis=1), jnp.concatenate([yh, yl, yh], axis=0))
        return ([z[:N, s * N:(s + 1) * N] for s in range(S)],
                [z[N:, s * N:(s + 1) * N] for s in range(S)])

    forward_halo(0)
    for k in range(K):
        assemble(k)
        if k + 1 < K:
            forward_halo(k + 1)
        if k == 0:
            fetch_probe.wait()
        exit_re, exit_im = [], []
        for s in range(S):
            tr, ti = window(k, s, 0), window(k, s, 1)
            patch[k, s, 0] = tr
            patch[k, s, 1] = ti
            if k == 0:
                wr, wi = probe[0], probe[1]
            else:
                wr, wi = wave[k - 1, s, 0], wave[k - 1, s, 1]
            exit_re.append(wr * tr - wi * ti)
            exit_im.append(wr * ti + wi * tr)
        if k + 1 < K:
            next_re, next_im = sandwich(exit_re, exit_im, 0, 1)
            for s in range(S):
                wave[k, s, 0] = next_re[s]
                wave[k, s, 1] = next_im[s]
        else:
            far_re, far_im = sandwich(exit_re, exit_im, 2, 3)

    fetch_meas.wait()
    grad_re, grad_im = [], []
    for s in range(S):
        amplitude = jnp.sqrt(far_re[s] * far_re[s] + far_im[s] * far_im[s] + 1.0)
        factor = (2.0 * live[s]) * (amplitude - meas[0, 0, s]) / amplitude
        grad_re.append(factor * far_re[s])
        grad_im.append(factor * far_im[s])

    def fold_columns(k):
        receive("gcol", k)
        left, right = g_in[k, 0], g_in[k, 1]
        mask = jnp.concatenate([low, low], axis=0)
        add_re = jnp.where(mask, left, turn(right))
        add_im = jnp.where(mask, turn(left), right)
        for p, add in ((0, add_re), (1, add_im)):
            total = padded[k, p, 0] + add
            m_send[k, 0, p] = total[:H]
            m_send[k, 1, p] = total[H + N:]
            out[k, p] = total[H:H + N]
        send("grow", k)

    h1 = 2 * N // C
    owners = min(R, h1 // 8)
    h2 = h1 // owners

    def piece(index, size):
        return pl.ds(pl.multiple_of(index * size, 8), size)

    def exchange(me, peer, src, dst, send_sem, recv_sem, device):
        return pltpu.make_async_remote_copy(
            src_ref=src, dst_ref=dst, send_sem=send_sem.at[peer], recv_sem=recv_sem.at[me],
            device_id=device, device_id_type=MESH)

    def col_scatter(me, peer):
        return exchange(me, peer, pg.at[piece(peer, h1)], s1.at[me], as_sem.at[0], ar_sem.at[0], (r, peer))

    def row_scatter(me, peer):
        return exchange(me, peer, q1.at[piece(peer, h2)], s2.at[me], bs_sem.at[0], br_sem.at[0], (peer, c))

    def row_gather(me, peer):
        return exchange(me, peer, q2, f2.at[piece(me, h2)], bs_sem.at[1], br_sem.at[1], (peer, c))

    def pg_piece(me):
        return pg_h.at[(me * h1) // N, piece(lax.rem(me, N // h1), h1)]

    def col_gather(me, peer):
        return exchange(me, peer, f2, pg_piece(me), as_sem.at[1], ar_sem.at[1], (r, peer))

    def when_owner(index, action):
        if owners == R:
            action()
        else:
            pl.when(index < owners)(action)

    col_peers = [lax.rem(c + j, C) for j in range(1, C)]
    row_peers = [lax.rem(r + j, R) for j in range(1, R)]

    def start_probe(re, im):
        pg[pl.ds(0, N), :] = sum(re)
        pg[pl.ds(N, N), :] = sum(im)
        for peer in col_peers:
            col_scatter(c, peer).start()

    for k in range(K - 1, -1, -1):
        right, left = (3, 2) if k == K - 1 else (1, 0)
        ge_re, ge_im = sandwich(grad_re, grad_im, right, left)
        new_re, new_im = [], []
        for s in range(S):
            tr, ti = patch[k, s, 0], patch[k, s, 1]
            new_re.append(tr * ge_re[s] + ti * ge_im[s])
            new_im.append(tr * ge_im[s] - ti * ge_re[s])
        grad_re, grad_im = new_re, new_im
        if k == 0:
            start_probe(grad_re, grad_im)
        for s in range(S):
            if k == 0:
                wr, wi = probe[0], probe[1]
            else:
                wr, wi = wave[k - 1, s, 0], wave[k - 1, s, 1]
            parts = (wr * ge_re[s] + wi * ge_im[s], wr * ge_im[s] - wi * ge_re[s])
            for p in range(2):
                moved = pltpu.roll(parts[p], xs[s], 1)
                zpad[s, p, 0, pl.ds(N, N), :] = jnp.where(lane >= xs[s], moved, 0.0)
                zpad[s, p, 1, pl.ds(N, N), :] = jnp.where(lane < xs[s], moved, 0.0)
        halves = []
        for p in range(2):
            halves.append([sum(zpad[s, p, h, pl.ds(N - ys[s], 2 * N), :] for s in range(S))
                           for h in range(2)])
        (re_lo, re_hi), (im_lo, im_hi) = halves
        mask = jnp.concatenate([low, low], axis=0)
        g_send[k, 0] = jnp.where(mask, re_lo, turn(im_lo))
        g_send[k, 1] = jnp.where(mask, turn(re_hi), im_hi)
        send("gcol", k)
        padded[k, 0, 0] = turn(jnp.where(mask, re_hi, re_lo))
        padded[k, 1, 0] = turn(jnp.where(mask, im_hi, im_lo))
        if k + 1 < K:
            fold_columns(k + 1)

    s1[c] = pg[piece(c, h1), :]
    for peer in col_peers:
        col_scatter(peer, c).wait_recv()
    q1[...] = sum(s1[j] for j in range(C))
    for peer in row_peers:
        when_owner(peer, lambda: row_scatter(r, peer).start())
    fold_columns(0)

    def reduce_rows():
        s2[r] = q1[piece(r, h2), :]
        for peer in row_peers:
            row_scatter(peer, r).wait_recv()
        total = sum(s2[j] for j in range(R))
        q2[...] = total
        f2[piece(r, h2), :] = total
        for peer in row_peers:
            row_gather(r, peer).start()

    when_owner(r, reduce_rows)
    for peer in row_peers:
        when_owner(peer, lambda: row_gather(peer, r).wait_recv())
    for peer in col_peers:
        col_gather(c, peer).start()
    keep = pltpu.make_async_copy(f2, pg_piece(c), local_sem.at[K + 3])
    keep.start()

    store_out = [pltpu.make_async_copy(out.at[k], out_h.at[k], local_sem.at[K + 4 + k]) for k in range(K)]
    for k in range(K - 1, -1, -1):
        receive("grow", k)
        for p in range(2):
            out[k, p, pl.ds(0, H), :] += m_in[k, 0, p]
            out[k, p, pl.ds(H, H), :] += m_in[k, 1, p]
        store_out[k].start()

    for peer in col_peers:
        col_gather(peer, c).wait_recv()
    sent()
    for peer in col_peers:
        col_scatter(c, peer).wait_send()
        col_gather(c, peer).wait_send()
    for peer in row_peers:
        when_owner(peer, lambda: row_scatter(r, peer).wait_send())
    for peer in row_peers:
        when_owner(r, lambda: row_gather(r, peer).wait_send())
    for store in [keep] + store_out:
        store.wait()


def copy_kernel(grad, probe_grad, grad_out, probe_out, grad_held, probe_held, in_sem, out_sem):
    K = grad.shape[0]
    pieces = [(grad.at[k], grad_held.at[k], grad_out.at[k]) for k in range(K)]
    pieces.append((probe_grad, probe_held, probe_out))
    loads = [pltpu.make_async_copy(src, held, in_sem.at[i]) for i, (src, held, _) in enumerate(pieces)]
    stores = [pltpu.make_async_copy(held, dst, out_sem.at[i]) for i, (_, held, dst) in enumerate(pieces)]
    for load in loads:
        load.start()
    for load, store in zip(loads, stores):
        load.wait()
        store.start()
    for store in stores:
        store.wait()


def per_device(R, C, object_field, probe_wave, positions, counts, measured):
    K, _, N, _ = object_field.shape
    S = measured.shape[2]
    H = N // 2
    f32 = jnp.float32
    h1 = 2 * N // C
    owners = min(R, h1 // 8)
    h2 = h1 // owners
    hbm = pl.BlockSpec(memory_space=pltpu.HBM)
    smem = pl.BlockSpec(memory_space=pltpu.SMEM)
    dma = pltpu.SemaphoreType.DMA
    grad, probe_grad = pl.pallas_call(
        functools.partial(kernel, R, C),
        out_shape=(jax.ShapeDtypeStruct(object_field.shape, f32), jax.ShapeDtypeStruct(probe_wave.shape, f32)),
        in_specs=[smem, smem, hbm, hbm, hbm, hbm],
        out_specs=(hbm, hbm),
        scratch_shapes=[
            pltpu.VMEM(object_field.shape, f32),
            pltpu.VMEM(probe_wave.shape, f32),
            pltpu.VMEM(measured.shape, f32),
            pltpu.VMEM((2, 2, N, N), f32),
            pltpu.VMEM((4, 2, 2 * N, 2 * N), jnp.bfloat16),
            pltpu.VMEM(object_field.shape, f32),
            pltpu.VMEM((K, 2, 2, H, N), f32),
            pltpu.VMEM((K, 2, 2, N, N), f32),
            pltpu.VMEM((K, 2, 2, N, N), f32),
            pltpu.VMEM((K, 2, 2, 2 * N, N), f32),
            pltpu.VMEM((K, S, 2, N, N), f32),
            pltpu.VMEM((K - 1, S, 2, N, N), f32),
            pltpu.VMEM((S, 2, 2, 3 * N, N), f32),
            pltpu.VMEM((K, 2, 2 * N, N), f32),
            pltpu.VMEM((K, 2, 2 * N, N), f32),
            pltpu.VMEM((K, 2, 2, H, N), f32),
            pltpu.VMEM((K, 2, 2, H, N), f32),
            pltpu.VMEM((2 * N, N), f32),
            pltpu.VMEM((C, h1, N), f32),
            pltpu.VMEM((h1, N), f32),
            pltpu.VMEM((R, h2, N), f32),
            pltpu.VMEM((h2, N), f32),
            pltpu.VMEM((h1, N), f32),
            dma((5, K, 2)), dma((5, K, 2)),
            dma((2, C)), dma((2, C)),
            dma((2, R)), dma((2, R)),
            dma((2 * K + 4,)),
        ],
        compiler_params=pltpu.CompilerParams(
            collective_id=0, has_side_effects=True, vmem_limit_bytes=63 * 1024 * 1024),
    )(positions, counts, object_field, probe_wave, measured, jnp.asarray(tables(N)))
    return pl.pallas_call(
        copy_kernel,
        out_shape=(jax.ShapeDtypeStruct(grad.shape, f32), jax.ShapeDtypeStruct(probe_grad.shape, f32)),
        in_specs=[hbm, hbm],
        out_specs=(hbm, hbm),
        scratch_shapes=[
            pltpu.VMEM(grad.shape, f32), pltpu.VMEM(probe_grad.shape, f32),
            dma((K + 1,)), dma((K + 1,)),
        ],
        compiler_params=pltpu.CompilerParams(vmem_limit_bytes=63 * 1024 * 1024),
    )(grad, probe_grad)


def solution(mesh):
    in_specs = (
        P(None, None, "row", "col"),
        P(),
        P("row", "col", None, None),
        P("row", "col"),
        P("row", "col", None, None, None),
    )
    out_specs = (P(None, None, "row", "col"), P())
    body = functools.partial(per_device, mesh.shape["row"], mesh.shape["col"])
    return jax.shard_map(body, mesh=mesh, in_specs=in_specs, out_specs=out_specs, check_vma=False)
```

```python
import functools
import math

import jax
import jax.numpy as jnp
import numpy as np
from jax import lax
from jax.experimental import pallas as pl
from jax.experimental.pallas import tpu as pltpu
from jax.sharding import PartitionSpec as P

FRESNEL = 0.01
MESH = pl.DeviceIdType.MESH


def tables(points):
    index = np.arange(points)
    dft = np.exp(-2j * math.pi * ((index[:, None] * index[None, :]) % points) / points) / math.sqrt(points)
    freq = np.where(index < points // 2, index, index - points).astype(np.float64)
    step = np.conj(dft) @ (np.exp(-1j * FRESNEL * freq**2)[:, None] * dft)
    return np.stack([np.stack([m.real, m.imag]) for m in (step, dft)]).astype(np.float32)


def split(x):
    high = x.astype(jnp.bfloat16)
    return high, (x - high.astype(jnp.float32)).astype(jnp.bfloat16)


def dot(a, b):
    return jnp.dot(a, b, preferred_element_type=jnp.float32)


def kernel(R, C, pos, cnt, obj_h, probe_h, meas_h, tab_h, out_h, pg_h,
           obj, probe, meas, tab, mats, out,
           row_in, col_send, col_in, padded, patch, wave, zpad, g_send, g_in, m_send, m_in,
           pg, s1, q1, s2, q2, f2,
           hs_sem, hr_sem, as_sem, ar_sem, bs_sem, br_sem, local_sem):
    K = obj_h.shape[0]
    N = obj_h.shape[-1]
    H = N // 2
    S = meas.shape[2]
    r = lax.axis_index("row")
    c = lax.axis_index("col")

    barrier = pltpu.get_barrier_semaphore()
    for j in range(1, R):
        pl.semaphore_signal(barrier, inc=1, device_id=(lax.rem(r + j, R), c), device_id_type=MESH)
    for j in range(1, C):
        pl.semaphore_signal(barrier, inc=1, device_id=(r, lax.rem(c + j, C)), device_id_type=MESH)

    fetch_obj = [pltpu.make_async_copy(obj_h.at[k], obj.at[k], local_sem.at[k]) for k in range(K)]
    fetch_probe = pltpu.make_async_copy(probe_h, probe, local_sem.at[K])
    fetch_meas = pltpu.make_async_copy(meas_h, meas, local_sem.at[K + 1])
    fetch_tab = pltpu.make_async_copy(tab_h, tab, local_sem.at[K + 2])
    for fetch in fetch_obj + [fetch_tab, fetch_probe, fetch_meas]:
        fetch.start()

    have = {"up": r > 0, "down": r < R - 1, "left": c > 0, "right": c < C - 1}
    where_to = {"up": (r - 1, c), "down": (r + 1, c), "left": (r, c - 1), "right": (r, c + 1)}
    back = {"up": "down", "down": "up", "left": "right", "right": "left"}
    slot = {"up": 0, "down": 1, "left": 0, "right": 1}

    def row_refs(k, side):
        rows = pl.ds(0, H) if side == "up" else pl.ds(H, H)
        return obj_h.at[k, :, rows, :], row_in.at[k, slot[back[side]]]

    def own_refs(k, side):
        return col_send.at[k, slot[side], 0], col_in.at[k, slot[back[side]], 0]

    def halo_refs(k, side):
        return col_send.at[k, slot[side], 1], col_in.at[k, slot[back[side]], 1]

    def gcol_refs(k, side):
        return g_send.at[k, slot[side]], g_in.at[k, slot[back[side]]]

    def grow_refs(k, side):
        return m_send.at[k, slot[side]], m_in.at[k, slot[back[side]]]

    kinds = {"row": (0, row_refs, ("up", "down")), "own": (1, own_refs, ("left", "right")),
             "halo": (2, halo_refs, ("left", "right")), "gcol": (3, gcol_refs, ("left", "right")),
             "grow": (4, grow_refs, ("up", "down"))}

    def copy_to(kind, k, side):
        number, refs, _ = kinds[kind]
        src, dst = refs(k, side)
        return pltpu.make_async_remote_copy(
            src_ref=src, dst_ref=dst,
            send_sem=hs_sem.at[number, k, slot[side]],
            recv_sem=hr_sem.at[number, k, slot[back[side]]],
            device_id=where_to[side], device_id_type=MESH)

    def send(kind, k):
        for side in kinds[kind][2]:
            @pl.when(have[side])
            def _():
                copy_to(kind, k, side).start()

    def receive(kind, k):
        for side in kinds[kind][2]:
            @pl.when(have[side])
            def _():
                number, refs, _ = kinds[kind]
                src, dst = refs(k, back[side])
                pltpu.make_async_remote_copy(
                    src_ref=src, dst_ref=dst,
                    send_sem=hs_sem.at[number, k, slot[back[side]]],
                    recv_sem=hr_sem.at[number, k, slot[side]],
                    device_id=where_to[side], device_id_type=MESH).wait_recv()

    def sent():
        for side in have:
            @pl.when(have[side])
            def _():
                for kind in kinds:
                    if side in kinds[kind][2]:
                        for k in range(K):
                            copy_to(kind, k, side).wait_send()

    lane = lax.broadcasted_iota(jnp.int32, (N, N), 1)
    low = lane < H
    low_h = lane[:H] < H

    def turn(x):
        return pltpu.roll(x, H, 1)

    pl.semaphore_wait(barrier, R + C - 2)
    send("row", 0)

    def pack_own(k):
        fetch_obj[k].wait()
        re, im = obj[k, 0], obj[k, 1]
        col_send[k, 0, 0] = jnp.where(low, re, turn(im))
        col_send[k, 1, 0] = jnp.where(low, turn(re), im)
        send("own", k)

    pack_own(0)
    send("row", 1)
    for side, buffers in (("up", (row_in, m_in)), ("down", (row_in, m_in)),
                          ("left", (col_in, g_in)), ("right", (col_in, g_in))):
        @pl.when(jnp.logical_not(have[side]))
        def _():
            for buffer in buffers:
                for k in range(K):
                    buffer[k, slot[side]] = jnp.zeros(buffer.shape[2:], jnp.float32)
    for s in range(S):
        for p in range(2):
            zpad[s, p, :, pl.ds(0, N), :] = jnp.zeros((2, N, N), jnp.float32)
            zpad[s, p, :, pl.ds(2 * N, N), :] = jnp.zeros((2, N, N), jnp.float32)

    fetch_tab.wait()
    for i in range(2):
        for part, (re, im) in enumerate(zip(split(tab[i, 0]), split(tab[i, 1]))):
            for form, (upper, lower) in enumerate(((im, -im), (-im, im))):
                mats[2 * i + form, part, pl.ds(0, N), pl.ds(0, N)] = re
                mats[2 * i + form, part, pl.ds(0, N), pl.ds(N, N)] = upper
                mats[2 * i + form, part, pl.ds(N, N), pl.ds(0, N)] = lower
                mats[2 * i + form, part, pl.ds(N, N), pl.ds(N, N)] = re
    pack_own(1)
    send("row", 2)

    ys = [jnp.clip(pos[0, 0, s, 0] - r * N, 0, N - 1) for s in range(S)]
    xs = [jnp.clip(pos[0, 0, s, 1] - c * N, 0, N - 1) for s in range(S)]
    live = [(s < cnt[0, 0]).astype(jnp.float32) for s in range(S)]

    def forward_halo(k):
        receive("row", k)
        for d in range(2):
            re, im = row_in[k, d, 0], row_in[k, d, 1]
            rows = pl.ds(d * H, H)
            col_send[k, 0, 1, rows, :] = jnp.where(low_h, re, turn(im))
            col_send[k, 1, 1, rows, :] = jnp.where(low_h, turn(re), im)
        send("halo", k)
        if k + 3 < K:
            send("row", k + 3)
        if k + 2 < K:
            pack_own(k + 2)

    def assemble(k):
        receive("own", k)
        receive("halo", k)
        for start, size, mid, part, begin in (
                (0, H, lambda p: row_in[k, 0, p], 1, 0),
                (H, N, lambda p: obj[k, p], 0, 0),
                (H + N, H, lambda p: row_in[k, 1, p], 1, H)):
            left = col_in[k, 0, part, pl.ds(begin, size), :]
            right = col_in[k, 1, part, pl.ds(begin, size), :]
            mask = low if size == N else low_h
            re, im = mid(0), mid(1)
            rows = pl.ds(start, size)
            padded[k, 0, 0, rows, :] = jnp.where(mask, left, turn(re))
            padded[k, 0, 1, rows, :] = turn(jnp.where(mask, right, re))
            padded[k, 1, 0, rows, :] = turn(jnp.where(mask, im, left))
            padded[k, 1, 1, rows, :] = jnp.where(mask, turn(im), right)

    def window(k, s, p):
        rows = pl.ds(ys[s], N)
        shift = lax.rem(N - xs[s], N)
        first = pltpu.roll(padded[k, p, 0, rows, :], shift, 1)
        second = pltpu.roll(padded[k, p, 1, rows, :], shift, 1)
        return jnp.where(lane < N - xs[s], first, second)

    def sandwich(res, ims, right, left):
        x = jnp.concatenate([jnp.concatenate([a, b], axis=1) for a, b in zip(res, ims)], axis=0)
        xh, xl = split(x)
        mh, ml = mats[right, 0], mats[right, 1]
        y = dot(jnp.concatenate([xh, xl, xh], axis=1), jnp.concatenate([mh, mh, ml], axis=0))
        y = jnp.concatenate(
            [jnp.concatenate([y[s * N:(s + 1) * N, :N] for s in range(S)], axis=1),
             jnp.concatenate([y[s * N:(s + 1) * N, N:] for s in range(S)], axis=1)], axis=0)
        yh, yl = split(y)
        mh, ml = mats[left, 0], mats[left, 1]
        z = dot(jnp.concatenate([mh, mh, ml], axis=1), jnp.concatenate([yh, yl, yh], axis=0))
        return ([z[:N, s * N:(s + 1) * N] for s in range(S)],
                [z[N:, s * N:(s + 1) * N] for s in range(S)])

    forward_halo(0)
    for k in range(K):
        assemble(k)
        if k + 1 < K:
            forward_halo(k + 1)
        if k == 0:
            fetch_probe.wait()
        exit_re, exit_im = [], []
        for s in range(S):
            tr, ti = window(k, s, 0), window(k, s, 1)
            patch[k, s, 0] = tr
            patch[k, s, 1] = ti
            if k == 0:
                wr, wi = probe[0], probe[1]
            else:
                wr, wi = wave[k - 1, s, 0], wave[k - 1, s, 1]
            exit_re.append(wr * tr - wi * ti)
            exit_im.append(wr * ti + wi * tr)
        if k + 1 < K:
            next_re, next_im = sandwich(exit_re, exit_im, 0, 1)
            for s in range(S):
                wave[k, s, 0] = next_re[s]
                wave[k, s, 1] = next_im[s]
        else:
            far_re, far_im = sandwich(exit_re, exit_im, 2, 3)

    fetch_meas.wait()
    grad_re, grad_im = [], []
    for s in range(S):
        amplitude = jnp.sqrt(far_re[s] * far_re[s] + far_im[s] * far_im[s] + 1.0)
        factor = (2.0 * live[s]) * (amplitude - meas[0, 0, s]) / amplitude
        grad_re.append(factor * far_re[s])
        grad_im.append(factor * far_im[s])

    def fold_columns(k):
        receive("gcol", k)
        left, right = g_in[k, 0], g_in[k, 1]
        mask = jnp.concatenate([low, low], axis=0)
        add_re = jnp.where(mask, left, turn(right))
        add_im = jnp.where(mask, turn(left), right)
        for p, add in ((0, add_re), (1, add_im)):
            total = padded[k, p, 0] + add
            m_send[k, 0, p] = total[:H]
            m_send[k, 1, p] = total[H + N:]
            out[k, p] = total[H:H + N]
        send("grow", k)

    h1 = 2 * N // C
    owners = min(R, h1 // 8)
    h2 = h1 // owners

    def piece(index, size):
        return pl.ds(pl.multiple_of(index * size, 8), size)

    def exchange(me, peer, src, dst, send_sem, recv_sem, device):
        return pltpu.make_async_remote_copy(
            src_ref=src, dst_ref=dst, send_sem=send_sem.at[peer], recv_sem=recv_sem.at[me],
            device_id=device, device_id_type=MESH)

    def col_scatter(me, peer):
        return exchange(me, peer, pg.at[piece(peer, h1)], s1.at[me], as_sem.at[0], ar_sem.at[0], (r, peer))

    def row_scatter(me, peer):
        return exchange(me, peer, q1.at[piece(peer, h2)], s2.at[me], bs_sem.at[0], br_sem.at[0], (peer, c))

    def row_gather(me, peer):
        return exchange(me, peer, q2, f2.at[piece(me, h2)], bs_sem.at[1], br_sem.at[1], (peer, c))

    def pg_piece(me):
        return pg_h.at[(me * h1) // N, piece(lax.rem(me, N // h1), h1)]

    def col_gather(me, peer):
        return exchange(me, peer, f2, pg_piece(me), as_sem.at[1], ar_sem.at[1], (r, peer))

    def when_owner(index, action):
        if owners == R:
            action()
        else:
            pl.when(index < owners)(action)

    col_peers = [lax.rem(c + j, C) for j in range(1, C)]
    row_peers = [lax.rem(r + j, R) for j in range(1, R)]

    def start_probe(re, im):
        pg[pl.ds(0, N), :] = sum(re)
        pg[pl.ds(N, N), :] = sum(im)
        for peer in col_peers:
            col_scatter(c, peer).start()

    for k in range(K - 1, -1, -1):
        right, left = (3, 2) if k == K - 1 else (1, 0)
        ge_re, ge_im = sandwich(grad_re, grad_im, right, left)
        new_re, new_im = [], []
        for s in range(S):
            tr, ti = patch[k, s, 0], patch[k, s, 1]
            new_re.append(tr * ge_re[s] + ti * ge_im[s])
            new_im.append(tr * ge_im[s] - ti * ge_re[s])
        grad_re, grad_im = new_re, new_im
        if k == 0:
            start_probe(grad_re, grad_im)
        for s in range(S):
            if k == 0:
                wr, wi = probe[0], probe[1]
            else:
                wr, wi = wave[k - 1, s, 0], wave[k - 1, s, 1]
            parts = (wr * ge_re[s] + wi * ge_im[s], wr * ge_im[s] - wi * ge_re[s])
            for p in range(2):
                moved = pltpu.roll(parts[p], xs[s], 1)
                zpad[s, p, 0, pl.ds(N, N), :] = jnp.where(lane >= xs[s], moved, 0.0)
                zpad[s, p, 1, pl.ds(N, N), :] = jnp.where(lane < xs[s], moved, 0.0)
        halves = []
        for p in range(2):
            halves.append([sum(zpad[s, p, h, pl.ds(N - ys[s], 2 * N), :] for s in range(S))
                           for h in range(2)])
        (re_lo, re_hi), (im_lo, im_hi) = halves
        mask = jnp.concatenate([low, low], axis=0)
        g_send[k, 0] = jnp.where(mask, re_lo, turn(im_lo))
        g_send[k, 1] = jnp.where(mask, turn(re_hi), im_hi)
        send("gcol", k)
        padded[k, 0, 0] = turn(jnp.where(mask, re_hi, re_lo))
        padded[k, 1, 0] = turn(jnp.where(mask, im_hi, im_lo))
        if k + 1 < K:
            fold_columns(k + 1)

    s1[c] = pg[piece(c, h1), :]
    for peer in col_peers:
        col_scatter(peer, c).wait_recv()
    q1[...] = sum(s1[j] for j in range(C))
    for peer in row_peers:
        when_owner(peer, lambda: row_scatter(r, peer).start())
    fold_columns(0)

    def reduce_rows():
        s2[r] = q1[piece(r, h2), :]
        for peer in row_peers:
            row_scatter(peer, r).wait_recv()
        total = sum(s2[j] for j in range(R))
        q2[...] = total
        f2[piece(r, h2), :] = total
        for peer in row_peers:
            row_gather(r, peer).start()

    when_owner(r, reduce_rows)
    for peer in row_peers:
        when_owner(peer, lambda: row_gather(peer, r).wait_recv())
    for peer in col_peers:
        col_gather(c, peer).start()
    keep = pltpu.make_async_copy(f2, pg_piece(c), local_sem.at[K + 3])
    keep.start()

    store_out = [pltpu.make_async_copy(out.at[k], out_h.at[k], local_sem.at[K + 4 + k]) for k in range(K)]
    for k in range(K - 1, -1, -1):
        receive("grow", k)
        for p in range(2):
            out[k, p, pl.ds(0, H), :] += m_in[k, 0, p]
            out[k, p, pl.ds(H, H), :] += m_in[k, 1, p]
        store_out[k].start()

    for peer in col_peers:
        col_gather(peer, c).wait_recv()
    sent()
    for peer in col_peers:
        col_scatter(c, peer).wait_send()
        col_gather(c, peer).wait_send()
    for peer in row_peers:
        when_owner(peer, lambda: row_scatter(r, peer).wait_send())
    for peer in row_peers:
        when_owner(r, lambda: row_gather(r, peer).wait_send())
    for store in [keep] + store_out:
        store.wait()


def copy_kernel(grad, probe_grad, grad_out, probe_out, grad_held, probe_held, in_sem, out_sem):
    K = grad.shape[0]
    pieces = [(grad.at[k], grad_held.at[k], grad_out.at[k]) for k in range(K)]
    pieces.append((probe_grad, probe_held, probe_out))
    loads = [pltpu.make_async_copy(src, held, in_sem.at[i]) for i, (src, held, _) in enumerate(pieces)]
    stores = [pltpu.make_async_copy(held, dst, out_sem.at[i]) for i, (_, held, dst) in enumerate(pieces)]
    for load in loads:
        load.start()
    for load, store in zip(loads, stores):
        load.wait()
        store.start()
    for store in stores:
        store.wait()


def per_device(R, C, object_field, probe_wave, positions, counts, measured):
    K, _, N, _ = object_field.shape
    S = measured.shape[2]
    H = N // 2
    f32 = jnp.float32
    h1 = 2 * N // C
    owners = min(R, h1 // 8)
    h2 = h1 // owners
    hbm = pl.BlockSpec(memory_space=pltpu.HBM)
    smem = pl.BlockSpec(memory_space=pltpu.SMEM)
    dma = pltpu.SemaphoreType.DMA
    grad, probe_grad = pl.pallas_call(
        functools.partial(kernel, R, C),
        out_shape=(jax.ShapeDtypeStruct(object_field.shape, f32), jax.ShapeDtypeStruct(probe_wave.shape, f32)),
        in_specs=[smem, smem, hbm, hbm, hbm, hbm],
        out_specs=(hbm, hbm),
        scratch_shapes=[
            pltpu.VMEM(object_field.shape, f32),
            pltpu.VMEM(probe_wave.shape, f32),
            pltpu.VMEM(measured.shape, f32),
            pltpu.VMEM((2, 2, N, N), f32),
            pltpu.VMEM((4, 2, 2 * N, 2 * N), jnp.bfloat16),
            pltpu.VMEM(object_field.shape, f32),
            pltpu.VMEM((K, 2, 2, H, N), f32),
            pltpu.VMEM((K, 2, 2, N, N), f32),
            pltpu.VMEM((K, 2, 2, N, N), f32),
            pltpu.VMEM((K, 2, 2, 2 * N, N), f32),
            pltpu.VMEM((K, S, 2, N, N), f32),
            pltpu.VMEM((K - 1, S, 2, N, N), f32),
            pltpu.VMEM((S, 2, 2, 3 * N, N), f32),
            pltpu.VMEM((K, 2, 2 * N, N), f32),
            pltpu.VMEM((K, 2, 2 * N, N), f32),
            pltpu.VMEM((K, 2, 2, H, N), f32),
            pltpu.VMEM((K, 2, 2, H, N), f32),
            pltpu.VMEM((2 * N, N), f32),
            pltpu.VMEM((C, h1, N), f32),
            pltpu.VMEM((h1, N), f32),
            pltpu.VMEM((R, h2, N), f32),
            pltpu.VMEM((h2, N), f32),
            pltpu.VMEM((h1, N), f32),
            dma((5, K, 2)), dma((5, K, 2)),
            dma((2, C)), dma((2, C)),
            dma((2, R)), dma((2, R)),
            dma((2 * K + 4,)),
        ],
        compiler_params=pltpu.CompilerParams(
            collective_id=0, has_side_effects=True, vmem_limit_bytes=63 * 1024 * 1024),
    )(positions, counts, object_field, probe_wave, measured, jnp.asarray(tables(N)))
    return pl.pallas_call(
        copy_kernel,
        out_shape=(jax.ShapeDtypeStruct(grad.shape, f32), jax.ShapeDtypeStruct(probe_grad.shape, f32)),
        in_specs=[hbm, hbm],
        out_specs=(hbm, hbm),
        scratch_shapes=[
            pltpu.VMEM(grad.shape, f32), pltpu.VMEM(probe_grad.shape, f32),
            dma((K + 1,)), dma((K + 1,)),
        ],
        compiler_params=pltpu.CompilerParams(vmem_limit_bytes=63 * 1024 * 1024),
    )(grad, probe_grad)


def solution(mesh):
    in_specs = (
        P(None, None, "row", "col"),
        P(),
        P("row", "col", None, None),
        P("row", "col"),
        P("row", "col", None, None, None),
    )
    out_specs = (P(None, None, "row", "col"), P())
    body = functools.partial(per_device, mesh.shape["row"], mesh.shape["col"])
    return jax.shard_map(body, mesh=mesh, in_specs=in_specs, out_specs=out_specs, check_vma=False)
```

```python
import functools
import math

import jax
import jax.numpy as jnp
import numpy as np
from jax import lax
from jax.experimental import pallas as pl
from jax.experimental.pallas import tpu as pltpu
from jax.sharding import PartitionSpec as P

FRESNEL = 0.01
MESH = pl.DeviceIdType.MESH


def tables(points):
    index = np.arange(points)
    dft = np.exp(-2j * math.pi * ((index[:, None] * index[None, :]) % points) / points) / math.sqrt(points)
    freq = np.where(index < points // 2, index, index - points).astype(np.float64)
    step = np.conj(dft) @ (np.exp(-1j * FRESNEL * freq**2)[:, None] * dft)
    return np.stack([np.stack([m.real, m.imag]) for m in (step, dft)]).astype(np.float32)


def split(x):
    high = x.astype(jnp.bfloat16)
    return high, (x - high.astype(jnp.float32)).astype(jnp.bfloat16)


def dot(a, b):
    return jnp.dot(a, b, preferred_element_type=jnp.float32)


def kernel(R, C, pos, cnt, obj_h, probe_h, meas_h, tab_h, out_h, pg_h,
           obj, probe, meas, tab, mats, out,
           row_in, col_send, col_in, padded, patch, wave, zpad, g_send, g_in, m_send, m_in,
           pg, s1, q1, s2, q2, f2,
           hs_sem, hr_sem, as_sem, ar_sem, bs_sem, br_sem, local_sem):
    K = obj_h.shape[0]
    N = obj_h.shape[-1]
    H = N // 2
    S = meas.shape[2]
    r = lax.axis_index("row")
    c = lax.axis_index("col")

    barrier = pltpu.get_barrier_semaphore()
    for j in range(1, R):
        pl.semaphore_signal(barrier, inc=1, device_id=(lax.rem(r + j, R), c), device_id_type=MESH)
    for j in range(1, C):
        pl.semaphore_signal(barrier, inc=1, device_id=(r, lax.rem(c + j, C)), device_id_type=MESH)

    fetch_obj = [pltpu.make_async_copy(obj_h.at[k], obj.at[k], local_sem.at[k]) for k in range(K)]
    fetch_probe = pltpu.make_async_copy(probe_h, probe, local_sem.at[K])
    fetch_meas = pltpu.make_async_copy(meas_h, meas, local_sem.at[K + 1])
    fetch_tab = pltpu.make_async_copy(tab_h, tab, local_sem.at[K + 2])
    for fetch in fetch_obj + [fetch_tab, fetch_probe, fetch_meas]:
        fetch.start()

    have = {"up": r > 0, "down": r < R - 1, "left": c > 0, "right": c < C - 1}
    where_to = {"up": (r - 1, c), "down": (r + 1, c), "left": (r, c - 1), "right": (r, c + 1)}
    back = {"up": "down", "down": "up", "left": "right", "right": "left"}
    slot = {"up": 0, "down": 1, "left": 0, "right": 1}

    def row_refs(k, side):
        rows = pl.ds(0, H) if side == "up" else pl.ds(H, H)
        return obj_h.at[k, :, rows, :], row_in.at[k, slot[back[side]]]

    def own_refs(k, side):
        return col_send.at[k, slot[side], 0], col_in.at[k, slot[back[side]], 0]

    def halo_refs(k, side):
        return col_send.at[k, slot[side], 1], col_in.at[k, slot[back[side]], 1]

    def gcol_refs(k, side):
        return g_send.at[k, slot[side]], g_in.at[k, slot[back[side]]]

    def grow_refs(k, side):
        return m_send.at[k, slot[side]], m_in.at[k, slot[back[side]]]

    kinds = {"row": (0, row_refs, ("up", "down")), "own": (1, own_refs, ("left", "right")),
             "halo": (2, halo_refs, ("left", "right")), "gcol": (3, gcol_refs, ("left", "right")),
             "grow": (4, grow_refs, ("up", "down"))}

    def copy_to(kind, k, side):
        number, refs, _ = kinds[kind]
        src, dst = refs(k, side)
        return pltpu.make_async_remote_copy(
            src_ref=src, dst_ref=dst,
            send_sem=hs_sem.at[number, k, slot[side]],
            recv_sem=hr_sem.at[number, k, slot[back[side]]],
            device_id=where_to[side], device_id_type=MESH)

    def send(kind, k):
        for side in kinds[kind][2]:
            @pl.when(have[side])
            def _():
                copy_to(kind, k, side).start()

    def receive(kind, k):
        for side in kinds[kind][2]:
            @pl.when(have[side])
            def _():
                number, refs, _ = kinds[kind]
                src, dst = refs(k, back[side])
                pltpu.make_async_remote_copy(
                    src_ref=src, dst_ref=dst,
                    send_sem=hs_sem.at[number, k, slot[back[side]]],
                    recv_sem=hr_sem.at[number, k, slot[side]],
                    device_id=where_to[side], device_id_type=MESH).wait_recv()

    def sent():
        for side in have:
            @pl.when(have[side])
            def _():
                for kind in kinds:
                    if side in kinds[kind][2]:
                        for k in range(K):
                            copy_to(kind, k, side).wait_send()

    lane = lax.broadcasted_iota(jnp.int32, (N, N), 1)
    low = lane < H
    low_h = lane[:H] < H

    def turn(x):
        return pltpu.roll(x, H, 1)

    pl.semaphore_wait(barrier, R + C - 2)
    send("row", 0)

    def pack_own(k):
        fetch_obj[k].wait()
        re, im = obj[k, 0], obj[k, 1]
        col_send[k, 0, 0] = jnp.where(low, re, turn(im))
        col_send[k, 1, 0] = jnp.where(low, turn(re), im)
        send("own", k)

    pack_own(0)
    for side, buffers in (("up", (row_in, m_in)), ("down", (row_in, m_in)),
                          ("left", (col_in, g_in)), ("right", (col_in, g_in))):
        @pl.when(jnp.logical_not(have[side]))
        def _():
            for buffer in buffers:
                for k in range(K):
                    buffer[k, slot[side]] = jnp.zeros(buffer.shape[2:], jnp.float32)
    for s in range(S):
        for p in range(2):
            zpad[s, p, :, pl.ds(0, N), :] = jnp.zeros((2, N, N), jnp.float32)
            zpad[s, p, :, pl.ds(2 * N, N), :] = jnp.zeros((2, N, N), jnp.float32)

    fetch_tab.wait()
    for i in range(2):
        for part, (re, im) in enumerate(zip(split(tab[i, 0]), split(tab[i, 1]))):
            for form, (upper, lower) in enumerate(((im, -im), (-im, im))):
                mats[2 * i + form, part, pl.ds(0, N), pl.ds(0, N)] = re
                mats[2 * i + form, part, pl.ds(0, N), pl.ds(N, N)] = upper
                mats[2 * i + form, part, pl.ds(N, N), pl.ds(0, N)] = lower
                mats[2 * i + form, part, pl.ds(N, N), pl.ds(N, N)] = re
    send("row", 1)
    pack_own(1)

    ys = [jnp.clip(pos[0, 0, s, 0] - r * N, 0, N - 1) for s in range(S)]
    xs = [jnp.clip(pos[0, 0, s, 1] - c * N, 0, N - 1) for s in range(S)]
    live = [(s < cnt[0, 0]).astype(jnp.float32) for s in range(S)]

    def forward_halo(k):
        receive("row", k)
        for d in range(2):
            re, im = row_in[k, d, 0], row_in[k, d, 1]
            rows = pl.ds(d * H, H)
            col_send[k, 0, 1, rows, :] = jnp.where(low_h, re, turn(im))
            col_send[k, 1, 1, rows, :] = jnp.where(low_h, turn(re), im)
        send("halo", k)
        if k + 2 < K:
            send("row", k + 2)
            pack_own(k + 2)

    def assemble(k):
        receive("own", k)
        receive("halo", k)
        for start, size, mid, part, begin in (
                (0, H, lambda p: row_in[k, 0, p], 1, 0),
                (H, N, lambda p: obj[k, p], 0, 0),
                (H + N, H, lambda p: row_in[k, 1, p], 1, H)):
            left = col_in[k, 0, part, pl.ds(begin, size), :]
            right = col_in[k, 1, part, pl.ds(begin, size), :]
            mask = low if size == N else low_h
            re, im = mid(0), mid(1)
            rows = pl.ds(start, size)
            padded[k, 0, 0, rows, :] = jnp.where(mask, left, turn(re))
            padded[k, 0, 1, rows, :] = turn(jnp.where(mask, right, re))
            padded[k, 1, 0, rows, :] = turn(jnp.where(mask, im, left))
            padded[k, 1, 1, rows, :] = jnp.where(mask, turn(im), right)

    def window(k, s, p):
        rows = pl.ds(ys[s], N)
        shift = lax.rem(N - xs[s], N)
        first = pltpu.roll(padded[k, p, 0, rows, :], shift, 1)
        second = pltpu.roll(padded[k, p, 1, rows, :], shift, 1)
        return jnp.where(lane < N - xs[s], first, second)

    def sandwich(res, ims, right, left):
        x = jnp.concatenate([jnp.concatenate([a, b], axis=1) for a, b in zip(res, ims)], axis=0)
        xh, xl = split(x)
        mh, ml = mats[right, 0], mats[right, 1]
        y = dot(jnp.concatenate([xh, xl, xh], axis=1), jnp.concatenate([mh, mh, ml], axis=0))
        y = jnp.concatenate(
            [jnp.concatenate([y[s * N:(s + 1) * N, :N] for s in range(S)], axis=1),
             jnp.concatenate([y[s * N:(s + 1) * N, N:] for s in range(S)], axis=1)], axis=0)
        yh, yl = split(y)
        mh, ml = mats[left, 0], mats[left, 1]
        z = dot(jnp.concatenate([mh, mh, ml], axis=1), jnp.concatenate([yh, yl, yh], axis=0))
        return ([z[:N, s * N:(s + 1) * N] for s in range(S)],
                [z[N:, s * N:(s + 1) * N] for s in range(S)])

    forward_halo(0)
    for k in range(K):
        assemble(k)
        if k + 1 < K:
            forward_halo(k + 1)
        if k == 0:
            fetch_probe.wait()
        exit_re, exit_im = [], []
        for s in range(S):
            tr, ti = window(k, s, 0), window(k, s, 1)
            patch[k, s, 0] = tr
            patch[k, s, 1] = ti
            if k == 0:
                wr, wi = probe[0], probe[1]
            else:
                wr, wi = wave[k - 1, s, 0], wave[k - 1, s, 1]
            exit_re.append(wr * tr - wi * ti)
            exit_im.append(wr * ti + wi * tr)
        if k + 1 < K:
            next_re, next_im = sandwich(exit_re, exit_im, 0, 1)
            for s in range(S):
                wave[k, s, 0] = next_re[s]
                wave[k, s, 1] = next_im[s]
        else:
            far_re, far_im = sandwich(exit_re, exit_im, 2, 3)

    fetch_meas.wait()
    grad_re, grad_im = [], []
    for s in range(S):
        amplitude = jnp.sqrt(far_re[s] * far_re[s] + far_im[s] * far_im[s] + 1.0)
        factor = (2.0 * live[s]) * (amplitude - meas[0, 0, s]) / amplitude
        grad_re.append(factor * far_re[s])
        grad_im.append(factor * far_im[s])

    def fold_columns(k):
        receive("gcol", k)
        left, right = g_in[k, 0], g_in[k, 1]
        mask = jnp.concatenate([low, low], axis=0)
        add_re = jnp.where(mask, left, turn(right))
        add_im = jnp.where(mask, turn(left), right)
        for p, add in ((0, add_re), (1, add_im)):
            total = padded[k, p, 0] + add
            m_send[k, 0, p] = total[:H]
            m_send[k, 1, p] = total[H + N:]
            out[k, p] = total[H:H + N]
        send("grow", k)

    h1 = 2 * N // C
    owners = min(R, h1 // 8)
    h2 = h1 // owners

    def piece(index, size):
        return pl.ds(pl.multiple_of(index * size, 8), size)

    def exchange(me, peer, src, dst, send_sem, recv_sem, device):
        return pltpu.make_async_remote_copy(
            src_ref=src, dst_ref=dst, send_sem=send_sem.at[peer], recv_sem=recv_sem.at[me],
            device_id=device, device_id_type=MESH)

    def col_scatter(me, peer):
        return exchange(me, peer, pg.at[piece(peer, h1)], s1.at[me], as_sem.at[0], ar_sem.at[0], (r, peer))

    def row_scatter(me, peer):
        return exchange(me, peer, q1.at[piece(peer, h2)], s2.at[me], bs_sem.at[0], br_sem.at[0], (peer, c))

    def row_gather(me, peer):
        return exchange(me, peer, q2, f2.at[piece(me, h2)], bs_sem.at[1], br_sem.at[1], (peer, c))

    def pg_piece(me):
        return pg_h.at[(me * h1) // N, piece(lax.rem(me, N // h1), h1)]

    def col_gather(me, peer):
        return exchange(me, peer, f2, pg_piece(me), as_sem.at[1], ar_sem.at[1], (r, peer))

    def when_owner(index, action):
        if owners == R:
            action()
        else:
            pl.when(index < owners)(action)

    col_peers = [lax.rem(c + j, C) for j in range(1, C)]
    row_peers = [lax.rem(r + j, R) for j in range(1, R)]

    def start_probe(re, im):
        pg[pl.ds(0, N), :] = sum(re)
        pg[pl.ds(N, N), :] = sum(im)
        for peer in col_peers:
            col_scatter(c, peer).start()

    for k in range(K - 1, -1, -1):
        right, left = (3, 2) if k == K - 1 else (1, 0)
        ge_re, ge_im = sandwich(grad_re, grad_im, right, left)
        new_re, new_im = [], []
        for s in range(S):
            tr, ti = patch[k, s, 0], patch[k, s, 1]
            new_re.append(tr * ge_re[s] + ti * ge_im[s])
            new_im.append(tr * ge_im[s] - ti * ge_re[s])
        grad_re, grad_im = new_re, new_im
        if k == 0:
            start_probe(grad_re, grad_im)
        for s in range(S):
            if k == 0:
                wr, wi = probe[0], probe[1]
            else:
                wr, wi = wave[k - 1, s, 0], wave[k - 1, s, 1]
            parts = (wr * ge_re[s] + wi * ge_im[s], wr * ge_im[s] - wi * ge_re[s])
            for p in range(2):
                moved = pltpu.roll(parts[p], xs[s], 1)
                zpad[s, p, 0, pl.ds(N, N), :] = jnp.where(lane >= xs[s], moved, 0.0)
                zpad[s, p, 1, pl.ds(N, N), :] = jnp.where(lane < xs[s], moved, 0.0)
        halves = []
        for p in range(2):
            halves.append([sum(zpad[s, p, h, pl.ds(N - ys[s], 2 * N), :] for s in range(S))
                           for h in range(2)])
        (re_lo, re_hi), (im_lo, im_hi) = halves
        mask = jnp.concatenate([low, low], axis=0)
        g_send[k, 0] = jnp.where(mask, re_lo, turn(im_lo))
        g_send[k, 1] = jnp.where(mask, turn(re_hi), im_hi)
        send("gcol", k)
        padded[k, 0, 0] = turn(jnp.where(mask, re_hi, re_lo))
        padded[k, 1, 0] = turn(jnp.where(mask, im_hi, im_lo))
        if k + 1 < K:
            fold_columns(k + 1)

    s1[c] = pg[piece(c, h1), :]
    for peer in col_peers:
        col_scatter(peer, c).wait_recv()
    q1[...] = sum(s1[j] for j in range(C))
    for peer in row_peers:
        when_owner(peer, lambda: row_scatter(r, peer).start())
    fold_columns(0)

    def reduce_rows():
        s2[r] = q1[piece(r, h2), :]
        for peer in row_peers:
            row_scatter(peer, r).wait_recv()
        total = sum(s2[j] for j in range(R))
        q2[...] = total
        f2[piece(r, h2), :] = total
        for peer in row_peers:
            row_gather(r, peer).start()

    when_owner(r, reduce_rows)
    for peer in row_peers:
        when_owner(peer, lambda: row_gather(peer, r).wait_recv())
    for peer in col_peers:
        col_gather(c, peer).start()
    keep = pltpu.make_async_copy(f2, pg_piece(c), local_sem.at[K + 3])
    keep.start()

    store_out = [pltpu.make_async_copy(out.at[k], out_h.at[k], local_sem.at[K + 4 + k]) for k in range(K)]
    for k in range(K - 1, -1, -1):
        receive("grow", k)
        for p in range(2):
            out[k, p, pl.ds(0, H), :] += m_in[k, 0, p]
            out[k, p, pl.ds(H, H), :] += m_in[k, 1, p]
        store_out[k].start()

    for peer in col_peers:
        col_gather(peer, c).wait_recv()
    sent()
    for peer in col_peers:
        col_scatter(c, peer).wait_send()
        col_gather(c, peer).wait_send()
    for peer in row_peers:
        when_owner(peer, lambda: row_scatter(r, peer).wait_send())
    for peer in row_peers:
        when_owner(r, lambda: row_gather(r, peer).wait_send())
    for store in [keep] + store_out:
        store.wait()


def copy_kernel(grad, probe_grad, grad_out, probe_out, grad_held, probe_held, in_sem, out_sem):
    K = grad.shape[0]
    pieces = [(grad.at[k], grad_held.at[k], grad_out.at[k]) for k in range(K)]
    pieces.append((probe_grad, probe_held, probe_out))
    loads = [pltpu.make_async_copy(src, held, in_sem.at[i]) for i, (src, held, _) in enumerate(pieces)]
    stores = [pltpu.make_async_copy(held, dst, out_sem.at[i]) for i, (_, held, dst) in enumerate(pieces)]
    for load in loads:
        load.start()
    for load, store in zip(loads, stores):
        load.wait()
        store.start()
    for store in stores:
        store.wait()


def per_device(R, C, object_field, probe_wave, positions, counts, measured):
    K, _, N, _ = object_field.shape
    S = measured.shape[2]
    H = N // 2
    f32 = jnp.float32
    h1 = 2 * N // C
    owners = min(R, h1 // 8)
    h2 = h1 // owners
    hbm = pl.BlockSpec(memory_space=pltpu.HBM)
    smem = pl.BlockSpec(memory_space=pltpu.SMEM)
    dma = pltpu.SemaphoreType.DMA
    grad, probe_grad = pl.pallas_call(
        functools.partial(kernel, R, C),
        out_shape=(jax.ShapeDtypeStruct(object_field.shape, f32), jax.ShapeDtypeStruct(probe_wave.shape, f32)),
        in_specs=[smem, smem, hbm, hbm, hbm, hbm],
        out_specs=(hbm, hbm),
        scratch_shapes=[
            pltpu.VMEM(object_field.shape, f32),
            pltpu.VMEM(probe_wave.shape, f32),
            pltpu.VMEM(measured.shape, f32),
            pltpu.VMEM((2, 2, N, N), f32),
            pltpu.VMEM((4, 2, 2 * N, 2 * N), jnp.bfloat16),
            pltpu.VMEM(object_field.shape, f32),
            pltpu.VMEM((K, 2, 2, H, N), f32),
            pltpu.VMEM((K, 2, 2, N, N), f32),
            pltpu.VMEM((K, 2, 2, N, N), f32),
            pltpu.VMEM((K, 2, 2, 2 * N, N), f32),
            pltpu.VMEM((K, S, 2, N, N), f32),
            pltpu.VMEM((K - 1, S, 2, N, N), f32),
            pltpu.VMEM((S, 2, 2, 3 * N, N), f32),
            pltpu.VMEM((K, 2, 2 * N, N), f32),
            pltpu.VMEM((K, 2, 2 * N, N), f32),
            pltpu.VMEM((K, 2, 2, H, N), f32),
            pltpu.VMEM((K, 2, 2, H, N), f32),
            pltpu.VMEM((2 * N, N), f32),
            pltpu.VMEM((C, h1, N), f32),
            pltpu.VMEM((h1, N), f32),
            pltpu.VMEM((R, h2, N), f32),
            pltpu.VMEM((h2, N), f32),
            pltpu.VMEM((h1, N), f32),
            dma((5, K, 2)), dma((5, K, 2)),
            dma((2, C)), dma((2, C)),
            dma((2, R)), dma((2, R)),
            dma((2 * K + 4,)),
        ],
        compiler_params=pltpu.CompilerParams(
            collective_id=0, has_side_effects=True, vmem_limit_bytes=63 * 1024 * 1024),
    )(positions, counts, object_field, probe_wave, measured, jnp.asarray(tables(N)))
    return pl.pallas_call(
        copy_kernel,
        out_shape=(jax.ShapeDtypeStruct(grad.shape, f32), jax.ShapeDtypeStruct(probe_grad.shape, f32)),
        in_specs=[hbm, hbm],
        out_specs=(hbm, hbm),
        scratch_shapes=[
            pltpu.VMEM(grad.shape, f32), pltpu.VMEM(probe_grad.shape, f32),
            dma((K + 1,)), dma((K + 1,)),
        ],
        compiler_params=pltpu.CompilerParams(vmem_limit_bytes=63 * 1024 * 1024),
    )(grad, probe_grad)


def solution(mesh):
    in_specs = (
        P(None, None, "row", "col"),
        P(),
        P("row", "col", None, None),
        P("row", "col"),
        P("row", "col", None, None, None),
    )
    out_specs = (P(None, None, "row", "col"), P())
    body = functools.partial(per_device, mesh.shape["row"], mesh.shape["col"])
    return jax.shard_map(body, mesh=mesh, in_specs=in_specs, out_specs=out_specs, check_vma=False)
```
